256 devices in a mesh: dp: 2 (over y_lo), ctx: 8 (over x, core), tensor: 16 (over y_hi, z).
Axes of the slice: x: 4, y: 4 (y_hi: 2, y_lo: 2; y = y_hi * 2 + y_lo), z: 8, core: 2. Of those that a mesh axis runs over, the one named last changes fastest.
Arguments:
- tokens: bfloat16 [4096, 4096], P(('dp', 'ctx', 'tensor')), parts along dimension 0, may hold values from -6 to 6
- norm_gain: float32 [4096], replicated, may hold values from 0.1 to 1.9
- in_weight: bfloat16 [4096, 3, 4096], P(None, None, 'tensor'), may hold values from -0.09375 to 0.09375
- short_filter: bfloat16 [3, 3, 4096], P(None, None, 'tensor'), may hold values from -3.5 to 3.5
- residues: float32 [16, 4096], P(None, 'tensor'), may hold values from -0.1 to 0.1
- decay_rate: float32 [16, 4096], P(None, 'tensor'), may hold values from 0.00012207031 to 0.0333333333
- skip_gain: float32 [4096], P('tensor'), may hold values from -4 to 4
- out_weight: bfloat16 [4096, 4096], P('tensor'), may hold values from -0.09375 to 0.09375
Outputs:
- layer_out: bfloat16 [4096, 4096], P(('dp', 'ctx', 'tensor')), parts along dimension 0
The draws below stay inside these ranges and needn't reach their ends.
There are 2 independent parts, one for each index of `dp`. The reference program is written for one: setup_inputs(seed, part) draws one part's arguments, and reference() takes and returns one part's arrays. A program takes and returns all parts, laid end to end along the dimension named above; an argument that names none is the same for every part. Nothing has to cross between parts.
All inputs are finite; a program needn't handle non-finite values.
Results may differ from the reference program's by a relative error of at most 0.025.
Values may be sent and summed in bfloat16 or wider, within the bound.
A program may use at most 128 MiB of HBM per device.

```python
import math
import jax
import jax.numpy as jnp
from jax import lax

D = 4096
MODES = 16
KSHORT = 3
SEQ = 2048
SUB = 128
N_TENSOR = 16


def draw_decay_rate(key, part):
    key = jax.random.fold_in(key, 11)
    key_pick, key_fast, key_slow = jax.random.split(key, 3)
    share = 0.5
    picker = jax.random.uniform(key_pick, (MODES, D), jnp.float32)
    fast_low = math.log(1.0 / 50.0)
    fast_high = math.log(1.0 / 30.0)
    slow_low = math.log(0.25 / SEQ)
    slow_high = math.log(2.0 / SEQ)
    fast_rate = jnp.exp(fast_low + jax.random.uniform(key_fast, (MODES, D), jnp.float32) * (fast_high - fast_low))
    slow_rate = jnp.exp(slow_low + jax.random.uniform(key_slow, (MODES, D), jnp.float32) * (slow_high - slow_low))
    return jnp.where(picker < share, fast_rate, slow_rate).astype(jnp.float32)


def levels(stream_key, dims, shards, smallest, largest):
    level, own = 1.0, jax.random.fold_in(stream_key, 6)
    for dim, parts in shards:
        steps = jnp.exp(jax.random.uniform(jax.random.fold_in(own, dim), (parts,), jnp.float32, smallest / len(shards), largest / len(shards)))
        level = level * jnp.repeat(steps, dims[dim] // parts).reshape([-1 if axis == dim else 1 for axis in range(len(dims))])
    return level


def centred(stream_key, shape, deviation, reach, cuts=(), kind=jnp.bfloat16):
    level = levels(stream_key, shape, cuts, -0.22, 0.18) if cuts else 1.0
    values = jax.random.normal(stream_key, shape, jnp.float32) * deviation * level
    return jnp.minimum(jnp.maximum(values, -reach), reach).astype(kind)


def setup_inputs(seed: int = 0, part: int = 0) -> dict:
    splits = jax.random.split(jax.random.key(seed), 9)
    part_splits = jax.random.split(jax.random.fold_in(splits[8], part), 9)
    return {
        "tokens": centred(part_splits[0], (SEQ, D), 1.0, 6.0, ((0, 128),)),
        "norm_gain": jnp.clip(1.0 + 0.18 * jax.random.normal(splits[1], (D,), jnp.float32), 0.1, 1.9),
        "in_weight": centred(splits[2], (D, 3, D), D ** -0.5, 0.09375, ((2, 16),)),
        "short_filter": centred(splits[3], (KSHORT, 3, D), KSHORT ** -0.5, 3.5, ((2, 16),)),
        "residues": centred(splits[4], (MODES, D), 0.02, 0.1, ((1, 16),), jnp.float32),
        "decay_rate": draw_decay_rate(jax.random.fold_in(splits[8], 71), part),
        "skip_gain": centred(splits[6], (D,), 1.0, 4.0, ((0, 16),), jnp.float32),
        "out_weight": centred(splits[7], (D, D), D ** -0.5, 0.09375, ((0, 16),)),
    }


EPSILON = 1e-06
PRECISE = lax.Precision.HIGHEST

def rms_rows(tokens, norm_gain):
    values = tokens.astype(jnp.float32)
    spread = lax.optimization_barrier(jnp.mean(values * values, axis=-1, keepdims=True))
    return (values * lax.rsqrt(spread + EPSILON) * norm_gain).astype(jnp.bfloat16)

def short_mix(padded, short_filter, row_count):
    tap_count = short_filter.shape[0]
    summed = jnp.zeros((row_count,) + padded.shape[1:], jnp.float32)
    for tap_index in range(tap_count):
        offset = tap_count - 1 - tap_index
        summed = summed + short_filter[tap_index].astype(jnp.float32) * padded[offset:offset + row_count].astype(jnp.float32)
    return summed

def mode_tables(residues, decay_rate, sub_width):
    lag_axis = jnp.arange(sub_width, dtype=jnp.float32)
    powers = jnp.exp(-decay_rate[:, None, :] * lag_axis[None, :, None])
    tap_sums = lax.optimization_barrier(jnp.sum(residues[:, None, :] * powers, axis=0))
    lag_index = (jnp.arange(sub_width, dtype=jnp.int32)[:, None] - jnp.arange(sub_width, dtype=jnp.int32)[None, :]).astype(jnp.int32)
    toeplitz = jnp.where((lag_index >= 0)[:, :, None], tap_sums[jnp.maximum(lag_index, 0)], jnp.float32(0.0))
    ends = powers[:, ::-1, :]
    carried = residues[:, None, :] * powers * jnp.exp(-decay_rate)[:, None, :]
    return (toeplitz, ends, carried)

def long_mix(signal, residues, decay_rate):
    toeplitz, ends, carried = mode_tables(residues, decay_rate, SUB)
    step_decay = jnp.exp(-decay_rate * SUB)
    blocks = signal.reshape(SEQ // SUB, SUB, signal.shape[1])

    def advance(carry_state, rows_now):
        within = jnp.einsum('tsc,sc->tc', toeplitz, rows_now, precision=PRECISE)
        carried_in = jnp.einsum('mtc,mc->tc', carried, carry_state, precision=PRECISE)
        carry_state = step_decay * carry_state + jnp.einsum('msc,sc->mc', ends, rows_now, precision=PRECISE)
        return (carry_state, within + carried_in)
    start_state = jnp.zeros((MODES, signal.shape[1]), jnp.float32)
    _, conv_rows = lax.scan(advance, start_state, blocks)
    return conv_rows.reshape(SEQ, signal.shape[1])

def reference(tokens, norm_gain, in_weight, short_filter, residues, decay_rate, skip_gain, out_weight):
    normed = rms_rows(tokens, norm_gain)
    flat_weight = in_weight.reshape(D, 3 * D)
    projected = jnp.dot(normed, flat_weight, preferred_element_type=jnp.float32).astype(jnp.bfloat16)
    padded = jnp.concatenate([jnp.zeros((KSHORT - 1, 3 * D), jnp.bfloat16), projected], axis=0)
    featured = short_mix(padded, short_filter.reshape(KSHORT, 3 * D), SEQ).reshape(SEQ, 3, D)
    signal = featured[:, 0, :] * featured[:, 2, :]
    long_out = long_mix(signal, residues, decay_rate)
    gated_rows = (featured[:, 1, :] * (long_out + skip_gain * signal)).astype(jnp.bfloat16)
    channels = D // N_TENSOR

    def add_group(summed, group):
        first_col = (group * channels).astype(jnp.int32)
        rows_now = lax.dynamic_slice_in_dim(gated_rows, first_col, channels, 1)
        weights_now = lax.dynamic_slice_in_dim(out_weight, first_col, channels, 0)
        term = jnp.dot(rows_now, weights_now, preferred_element_type=jnp.float32).astype(jnp.bfloat16)
        term = lax.optimization_barrier(term)
        return (summed + term.astype(jnp.float32), None)
    summed, _ = lax.scan(add_group, jnp.zeros((SEQ, D), jnp.float32), jnp.arange(N_TENSOR, dtype=jnp.int32))
    return (summed + tokens.astype(jnp.float32)).astype(jnp.bfloat16)
```

```python
import functools

import jax
import jax.numpy as jnp
from jax import lax
from jax.experimental import pallas as pl
from jax.experimental.pallas import tpu as pltpu
from jax.sharding import PartitionSpec as P

EPSILON = 1e-06
MESH = pl.DeviceIdType.MESH
SLICES = 4
SEGMENTS = 8
OWN = {(0, j): j - 1 for j in (1, 2, 3, 4)} | {(1, j): 3 + j for j in (1, 2, 3)}
OTH = {(0, j): 7 + j for j in (1, 2, 3, 4)} | {(1, j): 11 + j for j in (1, 2, 3)}
CROSS = 7
SLOTS = 15
REACH = (4, 3)


def kernel(
    sizes,
    tokens_hbm, gain_hbm, win_hbm, taps_hbm, res_hbm, rate_hbm, skip_hbm, wout_hbm,
    out_hbm,
    tok, gain, win, taps, res, rate, skip, wout,
    xg, proj, halo, sig, gate, dec, res3, far, step3, ends, state, states, inc,
    gated32, gated, part, land, outv,
    load_sem, ag_send, ag_recv, rs_send, rs_recv, halo_send, halo_recv, st_send, st_recv, out_sem,
):
    ring, n_ctx, rows, width = sizes
    block_rows = 2 * ring * rows
    cols = width // SLICES
    seg = block_rows // SEGMENTS
    channels = rate.shape[1]

    dp, ctx, tensor = lax.axis_index("dp"), lax.axis_index("ctx"), lax.axis_index("tensor")
    plane, z = tensor // ring, tensor % ring

    def at(ctx_now, plane_now, z_now):
        return (dp, ctx_now, plane_now * ring + z_now)

    partner = at(ctx, 1 - plane, z)

    loads = [
        pltpu.make_async_copy(source, target, load_sem.at[i])
        for i, (source, target) in enumerate(
            (
                (tokens_hbm, tok), (gain_hbm, gain), (rate_hbm, rate), (res_hbm, res),
                (taps_hbm, taps), (skip_hbm, skip), (win_hbm, win), (wout_hbm, wout),
            )
        )
    ]
    for load in loads:
        load.start()

    barrier = pltpu.get_barrier_semaphore()
    peers = [partner, at(ctx, plane, (z + 1) % ring), at(ctx, plane, (z + ring - 1) % ring)]
    peers += [at((ctx + o) % n_ctx, plane, z) for o in range(1, n_ctx)]
    for peer in peers:
        pl.semaphore_signal(barrier, inc=1, device_id=peer, device_id_type=MESH)

    def ring_at(k, chain, steps):
        sign = 1 - 2 * (k % 2) if chain == 0 else 2 * (k % 2) - 1
        return (z + sign * steps + 2 * ring) % ring

    def block(plane_now, z_now):
        return pl.ds(pl.multiple_of((plane_now * ring + z_now) * rows, rows), rows)

    def gather_copy(k, slot, plane_now, z_now, target):
        where = xg.at[k, block(plane_now, z_now), :]
        return pltpu.make_async_remote_copy(
            src_ref=where, dst_ref=where, send_sem=ag_send.at[k, slot], recv_sem=ag_recv.at[k, slot],
            device_id=target, device_id_type=MESH,
        )

    def scatter_copy(k, slot, plane_now, z_now, target):
        return pltpu.make_async_remote_copy(
            src_ref=part.at[k, block(plane_now, z_now), :], dst_ref=land.at[k, slot],
            send_sem=rs_send.at[k, slot], recv_sem=rs_recv.at[k, slot],
            device_id=target, device_id_type=MESH,
        )

    def each_slice(body):
        def step(k, carry):
            body(k)
            return carry

        lax.fori_loop(0, SLICES, step, 0)

    loads[0].wait()
    loads[1].wait()
    values = tok[...].astype(jnp.float32)
    spread = jnp.mean(values * values, axis=-1, keepdims=True)
    normed = (values * lax.rsqrt(spread + EPSILON) * gain[...]).astype(jnp.bfloat16)
    for k in range(SLICES):
        xg[k, block(plane, z), :] = normed[:, k * cols : (k + 1) * cols]
    pl.semaphore_wait(barrier, len(peers))

    def start_own(k):
        gather_copy(k, OWN[0, 1], plane, z, at(ctx, plane, ring_at(k, 0, 1))).start()
        gather_copy(k, OWN[1, 1], plane, z, at(ctx, plane, ring_at(k, 1, 1))).start()
        gather_copy(k, CROSS, plane, z, partner).start()

    each_slice(start_own)

    loads[2].wait()
    loads[3].wait()
    loads[4].wait()
    loads[5].wait()
    modes = rate.shape[0]
    for m in range(modes):
        step3[m] = jnp.broadcast_to(rate[m : m + 1, :], (SEGMENTS, channels))
        res3[m] = jnp.broadcast_to(res[m : m + 1, :], (SEGMENTS, channels))
    dec[...] = jnp.exp(-step3[...])

    def pass_own(j, chain):
        def body(k):
            origin = ring_at(k, chain, -j)
            gather_copy(k, OWN[chain, j], plane, origin, partner).wait_recv()
            gather_copy(k, OWN[chain, j + 1], plane, origin, at(ctx, plane, ring_at(k, chain, 1))).start()
            if j <= 2:
                gather_copy(k, OTH[chain, j], plane, origin, partner).start()

        return body

    def pass_other(j, chain):
        def body(k):
            origin = ring_at(k, chain, -j)
            gather_copy(k, OTH[chain, j], 1 - plane, origin, partner).wait_recv()
            gather_copy(k, OTH[chain, j + 1], 1 - plane, origin, at(ctx, plane, ring_at(k, chain, 1))).start()

        return body

    def both(*bodies):
        def body(k):
            for one in bodies:
                one(k)

        return body

    each_slice(both(pass_own(1, 0), pass_own(1, 1)))
    each_slice(both(pass_own(2, 0), pass_own(2, 1)))
    each_slice(both(pass_other(2, 0), pass_other(2, 1)))
    each_slice(both(pass_own(3, 0), pass_other(3, 0)))

    loads[6].wait()

    def project(k):
        for slot, plane_now, origin in (
            (OWN[1, 3], plane, ring_at(k, 1, -3)),
            (OTH[1, 3], 1 - plane, ring_at(k, 1, -3)),
            (OWN[0, 4], plane, ring_at(k, 0, -4)),
            (OTH[0, 4], 1 - plane, ring_at(k, 0, -4)),
            (CROSS, 1 - plane, z),
            (OTH[0, 1], 1 - plane, ring_at(k, 0, -1)),
            (OTH[1, 1], 1 - plane, ring_at(k, 1, -1)),
        ):
            gather_copy(k, slot, plane_now, origin, partner).wait_recv()
        depth = pl.ds(pl.multiple_of(k * cols, cols), cols)
        for g in range(3):
            group = pl.ds(g * channels, channels)
            product = jnp.dot(xg[k], win[g, depth, :], preferred_element_type=jnp.float32)
            product = product.reshape(SEGMENTS, seg, channels)

            @pl.when(k == 0)
            def _():
                proj[:, :, group] = product

            @pl.when(k > 0)
            def _():
                proj[:, :, group] += product

    each_slice(project)

    halo_copy = pltpu.make_async_remote_copy(
        src_ref=proj.at[SEGMENTS - 1, pl.ds(seg - 8, 8), :], dst_ref=halo,
        send_sem=halo_send, recv_sem=halo_recv,
        device_id=at((ctx + 1) % n_ctx, plane, z), device_id_type=MESH,
    )
    halo_copy.start()
    taps32 = taps[...].astype(jnp.float32)

    def short_mix(i, now, one, two):
        featured = []
        for g in range(3):
            group = slice(g * channels, (g + 1) * channels)
            featured.append(
                taps32[0, g : g + 1, :] * now[:, group]
                + taps32[1, g : g + 1, :] * one[:, group]
                + taps32[2, g : g + 1, :] * two[:, group]
            )
        sig[i] = featured[0] * featured[2]
        gate[i] = featured[1]

    def short_step(i, carry):
        short_mix(i, proj[:, i, :], proj[:, i - 1, :], proj[:, i - 2, :])
        return carry

    lax.fori_loop(2, seg, short_step, 0)

    halves = [pl.ds(first, 128) for first in range(0, channels, 128)]
    for half in halves:

        def end_step(i, carry, half=half):
            return dec[:, :, half] * carry + sig[i, :, half][None]

        ends[:, :, half] = lax.fori_loop(2, seg, end_step, jnp.zeros((modes, SEGMENTS, 128), jnp.float32))
    far[...] = jnp.exp(step3[...] * (-float(seg - 2)))

    halo_copy.wait_recv()
    first_row = lax.broadcasted_iota(jnp.int32, (SEGMENTS, 3 * channels), 0) == 0
    first_block = ctx == 0

    def entering(row, last):
        before = jnp.where(first_block, 0.0, halo[row : row + 1, :])
        return jnp.where(first_row, jnp.broadcast_to(before, last.shape), pltpu.roll(last, 1, 0))

    row_one = entering(7, proj[:, seg - 1, :])
    row_two = entering(6, proj[:, seg - 2, :])
    row_zero = proj[:, 0, :]
    short_mix(0, row_zero, row_one, row_two)
    short_mix(1, proj[:, 1, :], row_zero, row_one)

    lane = lax.broadcasted_iota(jnp.int32, (modes, SEGMENTS, 128), 1)
    for half in halves:
        total = ends[:, :, half] + far[:, :, half] * (dec[:, :, half] * sig[0, :, half][None] + sig[1, :, half][None])
        leap = far[:, :, half] * dec[:, :, half] * dec[:, :, half]
        for hop in (1, 2, 4):
            moved = pltpu.roll(total, hop, 1)
            total = total + jnp.where(lane >= hop, leap * moved, 0.0)
            leap = leap * leap
        ends[:, :, half] = total
    state[...] = ends[:, SEGMENTS - 1, :].astype(jnp.bfloat16)
    state_copies = [
        pltpu.make_async_remote_copy(
            src_ref=state, dst_ref=states.at[o - 1], send_sem=st_send.at[o - 1], recv_sem=st_recv.at[o - 1],
            device_id=at((ctx + o) % n_ctx, plane, z), device_id_type=MESH,
        )
        for o in range(1, n_ctx)
    ]
    for copy in state_copies:
        copy.start()
    segment = lax.broadcasted_iota(jnp.int32, (modes, SEGMENTS, channels), 1)
    step3[...] = jnp.exp(step3[...] * (segment.astype(jnp.float32) * (-float(seg))))
    for half in halves:
        ends[:, :, half] = jnp.where(lane >= 1, pltpu.roll(ends[:, :, half], 1, 1), 0.0)
    block_decay = jnp.exp(rate[...] * (-float(block_rows)))
    incoming = jnp.zeros(rate.shape, jnp.float32)
    for o in range(n_ctx - 1, 0, -1):
        state_copies[o - 1].wait_recv()
        incoming = block_decay * incoming + jnp.where(o <= ctx, states[o - 1].astype(jnp.float32), 0.0)
    inc[...] = incoming
    for m in range(modes):
        ends[m] = ends[m] + step3[m] * inc[m : m + 1, :]

    for half in halves:

        def long_step(i, carry, half=half):
            now = sig[i, :, half]
            carry = dec[:, :, half] * carry + now[None]
            mixed = jnp.sum(res3[:, :, half] * carry, axis=0)
            gated32[i, :, half] = gate[i, :, half] * (mixed + skip[:, half] * now)
            return carry

        lax.fori_loop(0, seg, long_step, ends[:, :, half])
    for s in range(SEGMENTS):
        gated[s * seg : (s + 1) * seg, :] = gated32[:, s, :].astype(jnp.bfloat16)

    loads[7].wait()

    def send_along(k, chain, j, plane_now, table):
        target = at(ctx, plane, ring_at(k, chain, -1))
        scatter_copy(k, table[chain, j], plane_now, ring_at(k, chain, -j), target).start()

    def send_across(k, chain, j):
        scatter_copy(k, OTH[chain, j], 1 - plane, ring_at(k, chain, -j), partner).start()

    def add(k, plane_now, z_now, slots):
        where = block(plane_now, z_now)
        total = part[k, where, :].astype(jnp.float32)
        for slot in slots:
            scatter_copy(k, slot, plane_now, z_now, partner).wait_recv()
            total = total + land[k, slot].astype(jnp.float32)
        part[k, where, :] = total.astype(jnp.bfloat16)

    def multiply(k):
        depth = pl.ds(pl.multiple_of(k * cols, cols), cols)
        part[k] = jnp.dot(gated[...], wout[:, depth], preferred_element_type=jnp.float32).astype(jnp.bfloat16)
        send_along(k, 0, 4, plane, OWN)
        send_along(k, 0, 4, 1 - plane, OTH)
        send_along(k, 1, 3, 1 - plane, OTH)
        send_along(k, 1, 3, plane, OWN)
        scatter_copy(k, CROSS, 1 - plane, z, partner).start()
        send_across(k, 0, 1)
        send_across(k, 1, 1)

    each_slice(multiply)

    def reduce_three(k):
        add(k, 1 - plane, ring_at(k, 0, -3), [OTH[0, 4]])
        send_along(k, 0, 3, 1 - plane, OTH)
        add(k, plane, ring_at(k, 0, -3), [OWN[0, 4]])
        send_along(k, 0, 3, plane, OWN)

    each_slice(reduce_three)

    def cross_two(k):
        for chain in (1, 0):
            add(k, 1 - plane, ring_at(k, chain, -2), [OTH[chain, 3]])
            send_across(k, chain, 2)

    each_slice(cross_two)

    def reduce_two(k):
        for chain in (1, 0):
            add(k, plane, ring_at(k, chain, -2), [OWN[chain, 3], OTH[chain, 2]])
            send_along(k, chain, 2, plane, OWN)

    each_slice(reduce_two)

    def reduce_one(k):
        for chain in (1, 0):
            add(k, plane, ring_at(k, chain, -1), [OTH[chain, 1], OWN[chain, 2]])
            send_along(k, chain, 1, plane, OWN)

    each_slice(reduce_one)

    for k in range(SLICES):
        total = part[k, block(plane, z), :].astype(jnp.float32)
        for slot in (CROSS, OWN[0, 1], OWN[1, 1]):
            scatter_copy(k, slot, plane, z, partner).wait_recv()
            total = total + land[k, slot].astype(jnp.float32)
        total = total + tok[:, k * cols : (k + 1) * cols].astype(jnp.float32)
        outv[:, k * cols : (k + 1) * cols] = total.astype(jnp.bfloat16)
    write = pltpu.make_async_copy(outv, out_hbm, out_sem)
    write.start()

    def drain(k):
        for slot in range(SLOTS):
            gather_copy(k, slot, plane, z, partner).wait_send()
            scatter_copy(k, slot, plane, z, partner).wait_send()

    each_slice(drain)
    halo_copy.wait_send()
    for copy in state_copies:
        copy.wait_send()
    write.wait()


def on_device(ring, n_ctx, tokens, norm_gain, in_weight, short_filter, residues, decay_rate, skip_gain, out_weight):
    rows, width = tokens.shape
    modes, channels = decay_rate.shape
    block_rows = 2 * ring * rows
    seg = block_rows // SEGMENTS
    cols = width // SLICES
    f32, bf16 = jnp.float32, jnp.bfloat16
    any_spec = pl.BlockSpec(memory_space=pl.ANY)
    table = pltpu.VMEM((modes, SEGMENTS, channels), f32)
    dma = pltpu.SemaphoreType.DMA
    return pl.pallas_call(
        functools.partial(kernel, (ring, n_ctx, rows, width)),
        out_shape=jax.ShapeDtypeStruct((rows, width), bf16),
        in_specs=[any_spec] * 8,
        out_specs=any_spec,
        scratch_shapes=[
            pltpu.VMEM((rows, width), bf16),
            pltpu.VMEM((1, width), f32),
            pltpu.VMEM((3, width, channels), bf16),
            pltpu.VMEM(short_filter.shape, bf16),
            pltpu.VMEM((modes, channels), f32),
            pltpu.VMEM((modes, channels), f32),
            pltpu.VMEM((1, channels), f32),
            pltpu.VMEM((channels, width), bf16),
            pltpu.VMEM((SLICES, block_rows, cols), bf16),
            pltpu.VMEM((SEGMENTS, seg, 3 * channels), f32),
            pltpu.VMEM((8, 3 * channels), f32),
            pltpu.VMEM((seg, SEGMENTS, channels), f32),
            pltpu.VMEM((seg, SEGMENTS, channels), f32),
            table, table, table, table, table,
            pltpu.VMEM((modes, channels), bf16),
            pltpu.VMEM((n_ctx - 1, modes, channels), bf16),
            pltpu.VMEM((modes, channels), f32),
            pltpu.VMEM((seg, SEGMENTS, channels), f32),
            pltpu.VMEM((block_rows, channels), bf16),
            pltpu.VMEM((SLICES, block_rows, cols), bf16),
            pltpu.VMEM((SLICES, SLOTS, rows, cols), bf16),
            pltpu.VMEM((rows, width), bf16),
            dma((8,)),
            dma((SLICES, SLOTS)), dma((SLICES, SLOTS)),
            dma((SLICES, SLOTS)), dma((SLICES, SLOTS)),
            dma, dma,
            dma((n_ctx - 1,)), dma((n_ctx - 1,)),
            dma,
        ],
        name="hyena_layer",
        cost_estimate=pl.CostEstimate(
            flops=2 * block_rows * width * channels * 4, bytes_accessed=8 * width * channels, transcendentals=0
        ),
        compiler_params=pltpu.CompilerParams(
            collective_id=0, has_side_effects=True, vmem_limit_bytes=48 * 2**20
        ),
    )(
        tokens, norm_gain.reshape(1, width), in_weight.transpose(1, 0, 2), short_filter,
        residues, decay_rate, skip_gain.reshape(1, channels), out_weight,
    )


def solution(mesh):
    ring, n_ctx = mesh.shape["tensor"] // 2, mesh.shape["ctx"]
    in_specs = (
        P(("dp", "ctx", "tensor"), None),
        P(),
        P(None, None, "tensor"),
        P(None, None, "tensor"),
        P(None, "tensor"),
        P(None, "tensor"),
        P("tensor"),
        P("tensor", None),
    )
    out_specs = P(("dp", "ctx", "tensor"), None)
    return jax.shard_map(
        functools.partial(on_device, ring, n_ctx),
        mesh=mesh, in_specs=in_specs, out_specs=out_specs, check_vma=False,
    )
```

```python
import functools

import jax
import jax.numpy as jnp
from jax import lax
from jax.experimental import pallas as pl
from jax.experimental.pallas import tpu as pltpu
from jax.sharding import PartitionSpec as P

EPSILON = 1e-06
MESH = pl.DeviceIdType.MESH
SLICES = 4
SEGMENTS = 8
OWN = {(0, j): j - 1 for j in (1, 2, 3, 4)} | {(1, j): 3 + j for j in (1, 2, 3)}
OTH = {(0, j): 7 + j for j in (1, 2, 3, 4)} | {(1, j): 11 + j for j in (1, 2, 3)}
CROSS = 7
SLOTS = 15
REACH = (4, 3)


def kernel(
    sizes,
    tokens_hbm, gain_hbm, win_hbm, taps_hbm, res_hbm, rate_hbm, skip_hbm, wout_hbm,
    out_hbm,
    tok, gain, win, taps, res, rate, skip, wout,
    xg, proj, halo, sig, gate, dec, res3, far, step3, ends, state, states, inc,
    gated32, gated, part, land, outv,
    load_sem, ag_send, ag_recv, rs_send, rs_recv, halo_send, halo_recv, st_send, st_recv, out_sem,
):
    ring, n_ctx, rows, width = sizes
    block_rows = 2 * ring * rows
    cols = width // SLICES
    seg = block_rows // SEGMENTS
    channels = rate.shape[1]

    dp, ctx, tensor = lax.axis_index("dp"), lax.axis_index("ctx"), lax.axis_index("tensor")
    plane, z = tensor // ring, tensor % ring

    def at(ctx_now, plane_now, z_now):
        return (dp, ctx_now, plane_now * ring + z_now)

    partner = at(ctx, 1 - plane, z)

    loads = [
        pltpu.make_async_copy(source, target, load_sem.at[i])
        for i, (source, target) in enumerate(
            (
                (tokens_hbm, tok), (gain_hbm, gain), (rate_hbm, rate), (res_hbm, res),
                (taps_hbm, taps), (skip_hbm, skip), (win_hbm, win), (wout_hbm, wout),
            )
        )
    ]
    for load in loads:
        load.start()

    barrier = pltpu.get_barrier_semaphore()
    peers = [partner, at(ctx, plane, (z + 1) % ring), at(ctx, plane, (z + ring - 1) % ring)]
    peers += [at((ctx + o) % n_ctx, plane, z) for o in range(1, n_ctx)]
    for peer in peers:
        pl.semaphore_signal(barrier, inc=1, device_id=peer, device_id_type=MESH)

    def ring_at(k, chain, steps):
        sign = 1 - 2 * (k % 2) if chain == 0 else 2 * (k % 2) - 1
        return (z + sign * steps + 2 * ring) % ring

    def block(plane_now, z_now):
        return pl.ds(pl.multiple_of((plane_now * ring + z_now) * rows, rows), rows)

    def gather_copy(k, slot, plane_now, z_now, target):
        where = xg.at[k, block(plane_now, z_now), :]
        return pltpu.make_async_remote_copy(
            src_ref=where, dst_ref=where, send_sem=ag_send.at[k, slot], recv_sem=ag_recv.at[k, slot],
            device_id=target, device_id_type=MESH,
        )

    def scatter_copy(k, slot, plane_now, z_now, target):
        return pltpu.make_async_remote_copy(
            src_ref=part.at[k, block(plane_now, z_now), :], dst_ref=land.at[k, slot],
            send_sem=rs_send.at[k, slot], recv_sem=rs_recv.at[k, slot],
            device_id=target, device_id_type=MESH,
        )

    def each_slice(body):
        def step(k, carry):
            body(k)
            return carry

        lax.fori_loop(0, SLICES, step, 0)

    loads[0].wait()
    loads[1].wait()
    values = tok[...].astype(jnp.float32)
    spread = jnp.mean(values * values, axis=-1, keepdims=True)
    normed = (values * lax.rsqrt(spread + EPSILON) * gain[...]).astype(jnp.bfloat16)
    for k in range(SLICES):
        xg[k, block(plane, z), :] = normed[:, k * cols : (k + 1) * cols]
    pl.semaphore_wait(barrier, len(peers))

    def start_own(k):
        gather_copy(k, OWN[0, 1], plane, z, at(ctx, plane, ring_at(k, 0, 1))).start()
        gather_copy(k, OWN[1, 1], plane, z, at(ctx, plane, ring_at(k, 1, 1))).start()
        gather_copy(k, CROSS, plane, z, partner).start()

    each_slice(start_own)

    loads[2].wait()
    loads[3].wait()
    loads[4].wait()
    loads[5].wait()
    modes = rate.shape[0]
    for m in range(modes):
        step3[m] = jnp.broadcast_to(rate[m : m + 1, :], (SEGMENTS, channels))
        res3[m] = jnp.broadcast_to(res[m : m + 1, :], (SEGMENTS, channels))
    dec[...] = jnp.exp(-step3[...])

    def arrived(k, slot, plane_now, origin):
        gather_copy(k, slot, plane_now, origin, partner).wait_recv()

    def along(k, chain, table, j, plane_now):
        target = at(ctx, plane, ring_at(k, chain, 1))
        gather_copy(k, table[chain, j], plane_now, ring_at(k, chain, 1 - j), target).start()

    def across(k, chain, j):
        gather_copy(k, OTH[chain, j], plane, ring_at(k, chain, -j), partner).start()

    def got_own(k, chain, j):
        arrived(k, OWN[chain, j], plane, ring_at(k, chain, -j))

    def got_other(k, chain, j):
        arrived(k, OTH[chain, j], 1 - plane, ring_at(k, chain, -j))

    def gather_one(k):
        got_own(k, 0, 1)
        along(k, 0, OWN, 2, plane)
        across(k, 0, 1)
        got_own(k, 1, 1)
        along(k, 1, OWN, 2, plane)

    def gather_two(k):
        got_own(k, 0, 2)
        along(k, 0, OWN, 3, plane)
        got_own(k, 1, 2)
        along(k, 1, OWN, 3, plane)
        across(k, 1, 2)

    def gather_three(k):
        got_own(k, 0, 3)
        along(k, 0, OWN, 4, plane)
        across(k, 0, 3)
        arrived(k, CROSS, 1 - plane, z)
        along(k, 1, OTH, 1, 1 - plane)
        got_own(k, 1, 3)
        across(k, 1, 3)

    def gather_four(k):
        got_other(k, 0, 1)
        along(k, 0, OTH, 2, 1 - plane)

    def gather_five(k):
        got_other(k, 0, 3)
        along(k, 0, OTH, 4, 1 - plane)

    for body in (gather_one, gather_two, gather_three, gather_four, gather_five):
        each_slice(body)

    loads[6].wait()

    def project(k):
        got_own(k, 0, 4)
        got_other(k, 1, 1)
        got_other(k, 1, 2)
        got_other(k, 0, 2)
        got_other(k, 1, 3)
        got_other(k, 0, 4)
        depth = pl.ds(pl.multiple_of(k * cols, cols), cols)
        for g in range(3):
            group = pl.ds(g * channels, channels)
            product = jnp.dot(xg[k], win[g, depth, :], preferred_element_type=jnp.float32)
            product = product.reshape(SEGMENTS, seg, channels)

            @pl.when(k == 0)
            def _():
                proj[:, :, group] = product

            @pl.when(k > 0)
            def _():
                proj[:, :, group] += product

    each_slice(project)

    halo_copy = pltpu.make_async_remote_copy(
        src_ref=proj.at[SEGMENTS - 1, pl.ds(seg - 8, 8), :], dst_ref=halo,
        send_sem=halo_send, recv_sem=halo_recv,
        device_id=at((ctx + 1) % n_ctx, plane, z), device_id_type=MESH,
    )
    halo_copy.start()
    taps32 = taps[...].astype(jnp.float32)

    def short_mix(i, now, one, two):
        featured = []
        for g in range(3):
            group = slice(g * channels, (g + 1) * channels)
            featured.append(
                taps32[0, g : g + 1, :] * now[:, group]
                + taps32[1, g : g + 1, :] * one[:, group]
                + taps32[2, g : g + 1, :] * two[:, group]
            )
        sig[i] = featured[0] * featured[2]
        gate[i] = featured[1]

    def short_step(i, carry):
        short_mix(i, proj[:, i, :], proj[:, i - 1, :], proj[:, i - 2, :])
        return carry

    lax.fori_loop(2, seg, short_step, 0)

    halves = [pl.ds(first, 128) for first in range(0, channels, 128)]
    for half in halves:

        def end_step(i, carry, half=half):
            return dec[:, :, half] * carry + sig[i, :, half][None]

        ends[:, :, half] = lax.fori_loop(2, seg, end_step, jnp.zeros((modes, SEGMENTS, 128), jnp.float32))
    far[...] = jnp.exp(step3[...] * (-float(seg - 2)))

    halo_copy.wait_recv()
    first_row = lax.broadcasted_iota(jnp.int32, (SEGMENTS, 3 * channels), 0) == 0
    first_block = ctx == 0

    def entering(row, last):
        before = jnp.where(first_block, 0.0, halo[row : row + 1, :])
        return jnp.where(first_row, jnp.broadcast_to(before, last.shape), pltpu.roll(last, 1, 0))

    row_one = entering(7, proj[:, seg - 1, :])
    row_two = entering(6, proj[:, seg - 2, :])
    row_zero = proj[:, 0, :]
    short_mix(0, row_zero, row_one, row_two)
    short_mix(1, proj[:, 1, :], row_zero, row_one)

    lane = lax.broadcasted_iota(jnp.int32, (modes, SEGMENTS, 128), 1)
    for half in halves:
        total = ends[:, :, half] + far[:, :, half] * (dec[:, :, half] * sig[0, :, half][None] + sig[1, :, half][None])
        leap = far[:, :, half] * dec[:, :, half] * dec[:, :, half]
        for hop in (1, 2, 4):
            moved = pltpu.roll(total, hop, 1)
            total = total + jnp.where(lane >= hop, leap * moved, 0.0)
            leap = leap * leap
        ends[:, :, half] = total
    state[...] = ends[:, SEGMENTS - 1, :].astype(jnp.bfloat16)
    state_copies = [
        pltpu.make_async_remote_copy(
            src_ref=state, dst_ref=states.at[o - 1], send_sem=st_send.at[o - 1], recv_sem=st_recv.at[o - 1],
            device_id=at((ctx + o) % n_ctx, plane, z), device_id_type=MESH,
        )
        for o in range(1, n_ctx)
    ]
    for copy in state_copies:
        copy.start()
    segment = lax.broadcasted_iota(jnp.int32, (modes, SEGMENTS, channels), 1)
    step3[...] = jnp.exp(step3[...] * (segment.astype(jnp.float32) * (-float(seg))))
    for half in halves:
        ends[:, :, half] = jnp.where(lane >= 1, pltpu.roll(ends[:, :, half], 1, 1), 0.0)
    block_decay = jnp.exp(rate[...] * (-float(block_rows)))
    incoming = jnp.zeros(rate.shape, jnp.float32)
    for o in range(n_ctx - 1, 0, -1):
        state_copies[o - 1].wait_recv()
        incoming = block_decay * incoming + jnp.where(o <= ctx, states[o - 1].astype(jnp.float32), 0.0)
    inc[...] = incoming
    for m in range(modes):
        ends[m] = ends[m] + step3[m] * inc[m : m + 1, :]

    for half in halves:

        def long_step(i, carry, half=half):
            now = sig[i, :, half]
            carry = dec[:, :, half] * carry + now[None]
            mixed = jnp.sum(res3[:, :, half] * carry, axis=0)
            gated32[i, :, half] = gate[i, :, half] * (mixed + skip[:, half] * now)
            return carry

        lax.fori_loop(0, seg, long_step, ends[:, :, half])
    for s in range(SEGMENTS):
        gated[s * seg : (s + 1) * seg, :] = gated32[:, s, :].astype(jnp.bfloat16)

    loads[7].wait()

    def send_along(k, chain, j, plane_now, table):
        target = at(ctx, plane, ring_at(k, chain, -1))
        scatter_copy(k, table[chain, j], plane_now, ring_at(k, chain, -j), target).start()

    def send_across(k, chain, j):
        scatter_copy(k, OTH[chain, j], 1 - plane, ring_at(k, chain, -j), partner).start()

    def add(k, plane_now, z_now, slots):
        where = block(plane_now, z_now)
        total = part[k, where, :].astype(jnp.float32)
        for slot in slots:
            scatter_copy(k, slot, plane_now, z_now, partner).wait_recv()
            total = total + land[k, slot].astype(jnp.float32)
        part[k, where, :] = total.astype(jnp.bfloat16)

    def multiply(k):
        depth = pl.ds(pl.multiple_of(k * cols, cols), cols)
        part[k] = jnp.dot(gated[...], wout[:, depth], preferred_element_type=jnp.float32).astype(jnp.bfloat16)
        send_across(k, 1, 3)
        send_along(k, 0, 4, 1 - plane, OTH)
        send_along(k, 0, 4, plane, OWN)
        send_along(k, 1, 1, 1 - plane, OTH)
        send_along(k, 0, 2, 1 - plane, OTH)

    each_slice(multiply)

    def reduce_one(k):
        add(k, 1 - plane, ring_at(k, 0, -3), [OTH[0, 4]])
        send_across(k, 0, 3)
        add(k, plane, ring_at(k, 1, -3), [OTH[1, 3]])
        send_along(k, 1, 3, plane, OWN)
        send_across(k, 1, 2)

    def reduce_two(k):
        add(k, plane, ring_at(k, 0, -3), [OWN[0, 4], OTH[0, 3]])
        send_along(k, 0, 3, plane, OWN)
        add(k, 1 - plane, ring_at(k, 0, -1), [OTH[0, 2]])
        send_across(k, 0, 1)

    def reduce_three(k):
        add(k, plane, ring_at(k, 1, -2), [OWN[1, 3], OTH[1, 2]])
        send_along(k, 1, 2, plane, OWN)
        add(k, plane, ring_at(k, 0, -2), [OWN[0, 3]])
        send_along(k, 0, 2, plane, OWN)
        add(k, 1 - plane, z, [OTH[1, 1]])
        scatter_copy(k, CROSS, 1 - plane, z, partner).start()

    def reduce_four(k):
        add(k, plane, ring_at(k, 1, -1), [OWN[1, 2]])
        send_along(k, 1, 1, plane, OWN)
        add(k, plane, ring_at(k, 0, -1), [OTH[0, 1], OWN[0, 2]])
        send_along(k, 0, 1, plane, OWN)

    for body in (reduce_one, reduce_two, reduce_three, reduce_four):
        each_slice(body)

    for k in range(SLICES):
        total = part[k, block(plane, z), :].astype(jnp.float32)
        for slot in (CROSS, OWN[0, 1], OWN[1, 1]):
            scatter_copy(k, slot, plane, z, partner).wait_recv()
            total = total + land[k, slot].astype(jnp.float32)
        total = total + tok[:, k * cols : (k + 1) * cols].astype(jnp.float32)
        outv[:, k * cols : (k + 1) * cols] = total.astype(jnp.bfloat16)
    write = pltpu.make_async_copy(outv, out_hbm, out_sem)
    write.start()

    def drain(k):
        for slot in range(SLOTS):
            gather_copy(k, slot, plane, z, partner).wait_send()
            scatter_copy(k, slot, plane, z, partner).wait_send()

    each_slice(drain)
    halo_copy.wait_send()
    for copy in state_copies:
        copy.wait_send()
    write.wait()


def on_device(ring, n_ctx, tokens, norm_gain, in_weight, short_filter, residues, decay_rate, skip_gain, out_weight):
    rows, width = tokens.shape
    modes, channels = decay_rate.shape
    block_rows = 2 * ring * rows
    seg = block_rows // SEGMENTS
    cols = width // SLICES
    f32, bf16 = jnp.float32, jnp.bfloat16
    any_spec = pl.BlockSpec(memory_space=pl.ANY)
    table = pltpu.VMEM((modes, SEGMENTS, channels), f32)
    dma = pltpu.SemaphoreType.DMA
    return pl.pallas_call(
        functools.partial(kernel, (ring, n_ctx, rows, width)),
        out_shape=jax.ShapeDtypeStruct((rows, width), bf16),
        in_specs=[any_spec] * 8,
        out_specs=any_spec,
        scratch_shapes=[
            pltpu.VMEM((rows, width), bf16),
            pltpu.VMEM((1, width), f32),
            pltpu.VMEM((3, width, channels), bf16),
            pltpu.VMEM(short_filter.shape, bf16),
            pltpu.VMEM((modes, channels), f32),
            pltpu.VMEM((modes, channels), f32),
            pltpu.VMEM((1, channels), f32),
            pltpu.VMEM((channels, width), bf16),
            pltpu.VMEM((SLICES, block_rows, cols), bf16),
            pltpu.VMEM((SEGMENTS, seg, 3 * channels), f32),
            pltpu.VMEM((8, 3 * channels), f32),
            pltpu.VMEM((seg, SEGMENTS, channels), f32),
            pltpu.VMEM((seg, SEGMENTS, channels), f32),
            table, table, table, table, table,
            pltpu.VMEM((modes, channels), bf16),
            pltpu.VMEM((n_ctx - 1, modes, channels), bf16),
            pltpu.VMEM((modes, channels), f32),
            pltpu.VMEM((seg, SEGMENTS, channels), f32),
            pltpu.VMEM((block_rows, channels), bf16),
            pltpu.VMEM((SLICES, block_rows, cols), bf16),
            pltpu.VMEM((SLICES, SLOTS, rows, cols), bf16),
            pltpu.VMEM((rows, width), bf16),
            dma((8,)),
            dma((SLICES, SLOTS)), dma((SLICES, SLOTS)),
            dma((SLICES, SLOTS)), dma((SLICES, SLOTS)),
            dma, dma,
            dma((n_ctx - 1,)), dma((n_ctx - 1,)),
            dma,
        ],
        name="hyena_layer",
        cost_estimate=pl.CostEstimate(
            flops=2 * block_rows * width * channels * 4, bytes_accessed=8 * width * channels, transcendentals=0
        ),
        compiler_params=pltpu.CompilerParams(
            collective_id=0, has_side_effects=True, vmem_limit_bytes=64 * 2**20
        ),
    )(
        tokens, norm_gain.reshape(1, width), in_weight.transpose(1, 0, 2), short_filter,
        residues, decay_rate, skip_gain.reshape(1, channels), out_weight,
    )


def solution(mesh):
    ring, n_ctx = mesh.shape["tensor"] // 2, mesh.shape["ctx"]
    in_specs = (
        P(("dp", "ctx", "tensor"), None),
        P(),
        P(None, None, "tensor"),
        P(None, None, "tensor"),
        P(None, "tensor"),
        P(None, "tensor"),
        P("tensor"),
        P("tensor", None),
    )
    out_specs = P(("dp", "ctx", "tensor"), None)
    return jax.shard_map(
        functools.partial(on_device, ring, n_ctx),
        mesh=mesh, in_specs=in_specs, out_specs=out_specs, check_vma=False,
    )
```

```python
import functools

import jax
import jax.numpy as jnp
from jax import lax
from jax.experimental import pallas as pl
from jax.experimental.pallas import tpu as pltpu
from jax.sharding import PartitionSpec as P

EPSILON = 1e-06
MESH = pl.DeviceIdType.MESH
SLICES = 4
SEGMENTS = 8
OWN = {(0, j): j - 1 for j in (1, 2, 3, 4)} | {(1, j): 3 + j for j in (1, 2, 3)}
OTH = {(0, j): 7 + j for j in (1, 2, 3, 4)} | {(1, j): 11 + j for j in (1, 2, 3)}
CROSS = 7
SLOTS = 15
REACH = (4, 3)


def kernel(
    sizes,
    tokens_hbm, gain_hbm, win_hbm, taps_hbm, res_hbm, rate_hbm, skip_hbm, wout_hbm,
    out,
    tok, gain, win, taps, res, rate, skip, wout,
    xg, proj, sig, gate, dec, res3, far, step3, ends, message, messages, rows32, before, heads, decays, inc,
    gated32, gated, part, land,
    load_sem, ag_send, ag_recv, rs_send, rs_recv, st_send, st_recv,
):
    ring, n_ctx, rows, width = sizes
    block_rows = 2 * ring * rows
    cols = width // SLICES
    seg = block_rows // SEGMENTS
    channels = rate.shape[1]

    dp, ctx, tensor = lax.axis_index("dp"), lax.axis_index("ctx"), lax.axis_index("tensor")
    plane, z = tensor // ring, tensor % ring

    def at(ctx_now, plane_now, z_now):
        return (dp, ctx_now, plane_now * ring + z_now)

    partner = at(ctx, 1 - plane, z)

    loads = [
        pltpu.make_async_copy(source, target, load_sem.at[i])
        for i, (source, target) in enumerate(
            (
                (tokens_hbm, tok), (gain_hbm, gain), (rate_hbm, rate), (res_hbm, res),
                (taps_hbm, taps), (skip_hbm, skip), (win_hbm, win), (wout_hbm, wout),
            )
        )
    ]
    for load in loads:
        load.start()

    barrier = pltpu.get_barrier_semaphore()
    peers = [partner, at(ctx, plane, (z + 1) % ring), at(ctx, plane, (z + ring - 1) % ring)]
    peers += [at((ctx + o) % n_ctx, plane, z) for o in range(1, n_ctx)]
    for peer in peers:
        pl.semaphore_signal(barrier, inc=1, device_id=peer, device_id_type=MESH)

    def ring_at(k, chain, steps):
        sign = 1 - 2 * (k % 2) if chain == 0 else 2 * (k % 2) - 1
        return (z + sign * steps + 2 * ring) % ring

    def block(plane_now, z_now):
        return pl.ds(pl.multiple_of((plane_now * ring + z_now) * rows, rows), rows)

    def gather_copy(k, slot, plane_now, z_now, target):
        where = xg.at[k, block(plane_now, z_now), :]
        return pltpu.make_async_remote_copy(
            src_ref=where, dst_ref=where, send_sem=ag_send.at[k, slot], recv_sem=ag_recv.at[k, slot],
            device_id=target, device_id_type=MESH,
        )

    def scatter_copy(k, slot, plane_now, z_now, target):
        return pltpu.make_async_remote_copy(
            src_ref=part.at[k, block(plane_now, z_now), :], dst_ref=land.at[k, slot],
            send_sem=rs_send.at[k, slot], recv_sem=rs_recv.at[k, slot],
            device_id=target, device_id_type=MESH,
        )

    def each_slice(body):
        def step(k, carry):
            body(k)
            return carry

        lax.fori_loop(0, SLICES, step, 0, unroll=True)

    loads[0].wait()
    loads[1].wait()
    values = tok[...].astype(jnp.float32)
    spread = jnp.mean(values * values, axis=-1, keepdims=True)
    normed = (values * lax.rsqrt(spread + EPSILON) * gain[...]).astype(jnp.bfloat16)
    for k in range(SLICES):
        xg[k, block(plane, z), :] = normed[:, k * cols : (k + 1) * cols]
    pl.semaphore_wait(barrier, len(peers))

    def start_own(k):
        gather_copy(k, OWN[0, 1], plane, z, at(ctx, plane, ring_at(k, 0, 1))).start()
        gather_copy(k, OWN[1, 1], plane, z, at(ctx, plane, ring_at(k, 1, 1))).start()
        gather_copy(k, CROSS, plane, z, partner).start()

    each_slice(start_own)

    loads[2].wait()
    loads[3].wait()
    loads[4].wait()
    loads[5].wait()
    modes = rate.shape[0]
    for m in range(modes):
        step3[m] = jnp.broadcast_to(rate[m : m + 1, :], (SEGMENTS, channels))
        res3[m] = jnp.broadcast_to(res[m : m + 1, :], (SEGMENTS, channels))
    dec[...] = jnp.exp(-step3[...])
    far[...] = jnp.exp(step3[...] * (-float(seg)))
    segment = lax.broadcasted_iota(jnp.int32, (modes, SEGMENTS, channels), 1)
    step3[...] = jnp.exp(step3[...] * (segment.astype(jnp.float32) * (-float(seg))))
    decays[0] = jnp.exp(-rate[...])
    decays[1] = jnp.exp(rate[...] * (-float(block_rows)))
    decays[2] = jnp.exp(rate[...] * (-float(block_rows - 2)))
    decays[3] = jnp.exp(rate[...])

    def arrived(k, slot, plane_now, origin):
        gather_copy(k, slot, plane_now, origin, partner).wait_recv()

    def along(k, chain, table, j, plane_now):
        target = at(ctx, plane, ring_at(k, chain, 1))
        gather_copy(k, table[chain, j], plane_now, ring_at(k, chain, 1 - j), target).start()

    def across(k, chain, j):
        gather_copy(k, OTH[chain, j], plane, ring_at(k, chain, -j), partner).start()

    def got_own(k, chain, j):
        arrived(k, OWN[chain, j], plane, ring_at(k, chain, -j))

    def got_other(k, chain, j):
        arrived(k, OTH[chain, j], 1 - plane, ring_at(k, chain, -j))

    def gather_one(k):
        got_own(k, 0, 1)
        along(k, 0, OWN, 2, plane)
        across(k, 0, 1)
        got_own(k, 1, 1)
        along(k, 1, OWN, 2, plane)

    def gather_two(k):
        got_own(k, 0, 2)
        along(k, 0, OWN, 3, plane)
        got_own(k, 1, 2)
        along(k, 1, OWN, 3, plane)
        across(k, 1, 2)

    def gather_three(k):
        got_own(k, 0, 3)
        along(k, 0, OWN, 4, plane)
        across(k, 0, 3)
        arrived(k, CROSS, 1 - plane, z)
        along(k, 1, OTH, 1, 1 - plane)
        got_own(k, 1, 3)
        across(k, 1, 3)

    def gather_four(k):
        got_other(k, 0, 1)
        along(k, 0, OTH, 2, 1 - plane)

    def gather_five(k):
        got_other(k, 0, 3)
        along(k, 0, OTH, 4, 1 - plane)

    for body in (gather_one, gather_two, gather_three, gather_four, gather_five):
        each_slice(body)

    loads[6].wait()

    def project(k):
        got_own(k, 0, 4)
        got_other(k, 1, 1)
        got_other(k, 1, 2)
        got_other(k, 0, 2)
        got_other(k, 1, 3)
        got_other(k, 0, 4)
        depth = pl.ds(pl.multiple_of(k * cols, cols), cols)
        for g in range(3):
            group = pl.ds(g * channels, channels)
            product = jnp.dot(xg[k], win[g, depth, :], preferred_element_type=jnp.float32)
            product = product.reshape(SEGMENTS, seg, channels)

            @pl.when(k == 0)
            def _():
                proj[:, :, group] = product

            @pl.when(k > 0)
            def _():
                proj[:, :, group] += product

    each_slice(project)

    taps32 = taps[...].astype(jnp.float32)

    def tap(j, g):
        return taps32[j, g : g + 1, :]

    def short_mix(i, now, one, two):
        featured = []
        for g in range(3):
            group = slice(g * channels, (g + 1) * channels)
            featured.append(tap(0, g) * now[:, group] + tap(1, g) * one[:, group] + tap(2, g) * two[:, group])
        sig[i] = featured[0] * featured[2]
        gate[i] = featured[1]

    def short_step(i, carry):
        short_mix(i, proj[:, i, :], proj[:, i - 1, :], proj[:, i - 2, :])
        return carry

    lax.fori_loop(2, seg, short_step, 0, unroll=6)

    first_row = lax.broadcasted_iota(jnp.int32, (SEGMENTS, 3 * channels), 0) == 0
    first_sig = lax.broadcasted_iota(jnp.int32, (SEGMENTS, channels), 0) == 0
    row_zero, row_next = proj[:, 0, :], proj[:, 1, :]
    row_one = pltpu.roll(proj[:, seg - 1, :], 1, 0)
    row_two = pltpu.roll(proj[:, seg - 2, :], 1, 0)
    short_mix(0, row_zero, row_one, row_two)
    short_mix(1, row_next, row_zero, row_one)
    sig[0] = jnp.where(first_sig, 0.0, sig[0])
    sig[1] = jnp.where(first_sig, 0.0, sig[1])

    halves = [pl.ds(first, 128) for first in range(0, channels, 128)]
    lane = lax.broadcasted_iota(jnp.int32, (modes, SEGMENTS, 128), 1)
    for half in halves:

        def end_step(i, carry, half=half):
            return dec[:, :, half] * carry + sig[i, :, half][None]

        total = lax.fori_loop(0, seg, end_step, jnp.zeros((modes, SEGMENTS, 128), jnp.float32), unroll=8)
        leap = far[:, :, half]
        for hop in (1, 2, 4):
            total = total + jnp.where(lane >= hop, leap * pltpu.roll(total, hop, 1), 0.0)
            leap = leap * leap
        ends[:, :, half] = total

    message[0:modes, :] = ends[:, SEGMENTS - 1, :].astype(jnp.bfloat16)
    last = [proj[SEGMENTS - 1, seg - 2 : seg - 1, :], proj[SEGMENTS - 1, seg - 1 : seg, :]]
    outer = [row_zero[0:1, :], row_next[0:1, :]] + last
    rows32[...] = jnp.zeros(rows32.shape, jnp.float32)
    for r, row in enumerate(outer):
        rows32[r : r + 1, :] = row[:, 0:channels]
        rows32[4 + r : 5 + r, :] = row[:, 2 * channels :]
    for r, row in enumerate(last):
        rows32[8 + r : 9 + r, :] = row[:, channels : 2 * channels]
    message[modes:, :] = rows32[...].astype(jnp.bfloat16)
    copies = [
        pltpu.make_async_remote_copy(
            src_ref=message, dst_ref=messages.at[o - 1], send_sem=st_send.at[o - 1], recv_sem=st_recv.at[o - 1],
            device_id=at((ctx + o) % n_ctx, plane, z), device_id_type=MESH,
        )
        for o in range(1, n_ctx)
    ]
    for copy in copies:
        copy.start()

    for half in halves:
        ends[:, :, half] = jnp.where(lane >= 1, pltpu.roll(ends[:, :, half], 1, 1), 0.0)

    def drain_gather(k):
        for slot in range(SLOTS):
            gather_copy(k, slot, plane, z, partner).wait_send()

    each_slice(drain_gather)

    for o in range(1, n_ctx):
        copies[o - 1].wait_recv()
        before[o - 1] = jnp.where(o <= ctx, messages[o - 1, modes:, :].astype(jnp.float32), 0.0)
    before[n_ctx - 1] = jnp.zeros(before.shape[1:], jnp.float32)
    before[n_ctx] = jnp.zeros(before.shape[1:], jnp.float32)

    def first_two(r, g):
        start, then = before[0:n_ctx, r, :], before[0:n_ctx, r + 1, :]
        two, one = before[1 : n_ctx + 1, r + 2, :], before[1 : n_ctx + 1, r + 3, :]
        return (
            tap(0, g) * start + tap(1, g) * one + tap(2, g) * two,
            tap(0, g) * then + tap(1, g) * start + tap(2, g) * one,
        )

    left, right = first_two(0, 0), first_two(4, 2)
    heads[0] = left[0] * right[0]
    heads[1] = left[1] * right[1]
    decay = decays[0]
    incoming = jnp.zeros(rate.shape, jnp.float32)
    for o in range(n_ctx - 1, 0, -1):
        ended = jnp.where(o <= ctx, messages[o - 1, 0:modes, :].astype(jnp.float32), 0.0)
        head = decay * heads[0, o - 1 : o, :] + heads[1, o - 1 : o, :]
        incoming = decays[1] * incoming + (ended + decays[2] * head)

    def halo(r):
        row = jnp.concatenate([before[0, r : r + 1, :], before[0, 8 + r - 2 : 9 + r - 2, :], before[0, 4 + r : 5 + r, :]], axis=1)
        return jnp.broadcast_to(row, (SEGMENTS, 3 * channels))

    row_one = jnp.where(first_row, halo(3), pltpu.roll(proj[:, seg - 1, :], 1, 0))
    row_two = jnp.where(first_row, halo(2), pltpu.roll(proj[:, seg - 2, :], 1, 0))
    row_zero = proj[:, 0, :]
    short_mix(0, row_zero, row_one, row_two)
    short_mix(1, proj[:, 1, :], row_zero, row_one)
    inc[0] = incoming
    inc[1] = incoming + decays[3] * (sig[0, 0:1, :] + decays[3] * sig[1, 0:1, :])
    first_sig = lax.broadcasted_iota(jnp.int32, (SEGMENTS, channels), 0) == 0
    for m in range(modes):
        ends[m] = ends[m] + step3[m] * jnp.where(first_sig, inc[0, m : m + 1, :], inc[1, m : m + 1, :])

    for half in halves:

        def long_step(i, carry, half=half):
            now = sig[i, :, half]
            carry = dec[:, :, half] * carry + now[None]
            mixed = jnp.sum(res3[:, :, half] * carry, axis=0)
            gated32[i, :, half] = gate[i, :, half] * (mixed + skip[:, half] * now)
            return carry

        lax.fori_loop(0, seg, long_step, ends[:, :, half], unroll=4)
    for s in range(SEGMENTS):
        gated[s * seg : (s + 1) * seg, :] = gated32[:, s, :].astype(jnp.bfloat16)

    loads[7].wait()

    def send_along(k, chain, j, plane_now, table):
        target = at(ctx, plane, ring_at(k, chain, -1))
        scatter_copy(k, table[chain, j], plane_now, ring_at(k, chain, -j), target).start()

    def send_across(k, chain, j):
        scatter_copy(k, OTH[chain, j], 1 - plane, ring_at(k, chain, -j), partner).start()

    def add(k, plane_now, z_now, slots):
        where = block(plane_now, z_now)
        total = part[k, where, :].astype(jnp.float32)
        for slot in slots:
            scatter_copy(k, slot, plane_now, z_now, partner).wait_recv()
            total = total + land[k, slot].astype(jnp.float32)
        part[k, where, :] = total.astype(jnp.bfloat16)

    def multiply(k):
        depth = pl.ds(pl.multiple_of(k * cols, cols), cols)
        part[k] = jnp.dot(gated[...], wout[:, depth], preferred_element_type=jnp.float32).astype(jnp.bfloat16)
        send_across(k, 1, 3)
        send_along(k, 0, 4, 1 - plane, OTH)
        send_along(k, 0, 4, plane, OWN)
        send_along(k, 1, 1, 1 - plane, OTH)
        send_along(k, 0, 2, 1 - plane, OTH)

    each_slice(multiply)

    def reduce_one(k):
        add(k, 1 - plane, ring_at(k, 0, -3), [OTH[0, 4]])
        send_across(k, 0, 3)
        add(k, plane, ring_at(k, 1, -3), [OTH[1, 3]])
        send_along(k, 1, 3, plane, OWN)
        send_across(k, 1, 2)

    def reduce_two(k):
        add(k, plane, ring_at(k, 0, -3), [OWN[0, 4], OTH[0, 3]])
        send_along(k, 0, 3, plane, OWN)
        add(k, 1 - plane, ring_at(k, 0, -1), [OTH[0, 2]])
        send_across(k, 0, 1)

    def reduce_three(k):
        add(k, plane, ring_at(k, 1, -2), [OWN[1, 3], OTH[1, 2]])
        send_along(k, 1, 2, plane, OWN)
        add(k, plane, ring_at(k, 0, -2), [OWN[0, 3]])
        send_along(k, 0, 2, plane, OWN)
        add(k, 1 - plane, z, [OTH[1, 1]])
        scatter_copy(k, CROSS, 1 - plane, z, partner).start()

    def reduce_four(k):
        add(k, plane, ring_at(k, 1, -1), [OWN[1, 2]])
        send_along(k, 1, 1, plane, OWN)
        add(k, plane, ring_at(k, 0, -1), [OTH[0, 1], OWN[0, 2]])
        send_along(k, 0, 1, plane, OWN)

    for body in (reduce_one, reduce_two, reduce_three, reduce_four):
        each_slice(body)

    late = (CROSS, OWN[0, 1], OWN[1, 1])

    def drain_scatter(k):
        for slot in range(SLOTS):
            if slot not in late:
                scatter_copy(k, slot, plane, z, partner).wait_send()

    each_slice(drain_scatter)
    for k in range(SLICES):
        columns = pl.ds(k * cols, cols)
        total = part[k, block(plane, z), :].astype(jnp.float32) + tok[:, columns].astype(jnp.float32)
        for slot in late:
            scatter_copy(k, slot, plane, z, partner).wait_recv()
            total = total + land[k, slot].astype(jnp.float32)
        out[:, columns] = total.astype(jnp.bfloat16)
    for k in range(SLICES):
        for slot in late:
            scatter_copy(k, slot, plane, z, partner).wait_send()
    for copy in copies:
        copy.wait_send()


def on_device(ring, n_ctx, tokens, norm_gain, in_weight, short_filter, residues, decay_rate, skip_gain, out_weight):
    rows, width = tokens.shape
    modes, channels = decay_rate.shape
    block_rows = 2 * ring * rows
    seg = block_rows // SEGMENTS
    cols = width // SLICES
    f32, bf16 = jnp.float32, jnp.bfloat16
    any_spec = pl.BlockSpec(memory_space=pl.ANY)
    table = pltpu.VMEM((modes, SEGMENTS, channels), f32)
    dma = pltpu.SemaphoreType.DMA
    return pl.pallas_call(
        functools.partial(kernel, (ring, n_ctx, rows, width)),
        out_shape=pltpu.VMEM((rows, width), bf16),
        in_specs=[any_spec] * 8,
        out_specs=pl.BlockSpec(memory_space=pltpu.VMEM),
        scratch_shapes=[
            pltpu.VMEM((rows, width), bf16),
            pltpu.VMEM((1, width), f32),
            pltpu.VMEM((3, width, channels), bf16),
            pltpu.VMEM(short_filter.shape, bf16),
            pltpu.VMEM((modes, channels), f32),
            pltpu.VMEM((modes, channels), f32),
            pltpu.VMEM((1, channels), f32),
            pltpu.VMEM((channels, width), bf16),
            pltpu.VMEM((SLICES, block_rows, cols), bf16),
            pltpu.VMEM((SEGMENTS, seg, 3 * channels), f32),
            pltpu.VMEM((seg, SEGMENTS, channels), f32),
            pltpu.VMEM((seg, SEGMENTS, channels), f32),
            table, table, table, table, table,
            pltpu.VMEM((modes + 16, channels), bf16),
            pltpu.VMEM((n_ctx - 1, modes + 16, channels), bf16),
            pltpu.VMEM((16, channels), f32),
            pltpu.VMEM((n_ctx + 1, 16, channels), f32),
            pltpu.VMEM((2, n_ctx, channels), f32),
            pltpu.VMEM((4, modes, channels), f32),
            pltpu.VMEM((2, modes, channels), f32),
            pltpu.VMEM((seg, SEGMENTS, channels), f32),
            pltpu.VMEM((block_rows, channels), bf16),
            pltpu.VMEM((SLICES, block_rows, cols), bf16),
            pltpu.VMEM((SLICES, SLOTS, rows, cols), bf16),
            dma((8,)),
            dma((SLICES, SLOTS)), dma((SLICES, SLOTS)),
            dma((SLICES, SLOTS)), dma((SLICES, SLOTS)),
            dma((n_ctx - 1,)), dma((n_ctx - 1,)),
        ],
        name="hyena_layer",
        cost_estimate=pl.CostEstimate(
            flops=2 * block_rows * width * channels * 4, bytes_accessed=8 * width * channels, transcendentals=0
        ),
        compiler_params=pltpu.CompilerParams(
            collective_id=0, has_side_effects=True, vmem_limit_bytes=60 * 2**20
        ),
    )(
        tokens, norm_gain.reshape(1, width), in_weight.transpose(1, 0, 2), short_filter,
        residues, decay_rate, skip_gain.reshape(1, channels), out_weight,
    )


def solution(mesh):
    ring, n_ctx = mesh.shape["tensor"] // 2, mesh.shape["ctx"]
    in_specs = (
        P(("dp", "ctx", "tensor"), None),
        P(),
        P(None, None, "tensor"),
        P(None, None, "tensor"),
        P(None, "tensor"),
        P(None, "tensor"),
        P("tensor"),
        P("tensor", None),
    )
    out_specs = P(("dp", "ctx", "tensor"), None)
    return jax.shard_map(
        functools.partial(on_device, ring, n_ctx),
        mesh=mesh, in_specs=in_specs, out_specs=out_specs, check_vma=False,
    )
```

```python
import functools

import jax
import jax.numpy as jnp
from jax import lax
from jax.experimental import pallas as pl
from jax.experimental.pallas import tpu as pltpu
from jax.sharding import PartitionSpec as P

EPSILON = 1e-06
MESH = pl.DeviceIdType.MESH
SLICES = 4
SEGMENTS = 8
STEPS = (1, 2, 3, 4, -1, -2, -3)
GATHER_FROM = (
    {-3: -2, -2: -1, -1: 0, 0: "x", 1: "x", 2: 1, 3: "x", 4: 3},
    {-3: -2, -2: -1, -1: "x", 0: "x", 1: 0, 2: "x", 3: "x", 4: "x"},
    {-3: -2, -2: "x", -1: "x", 0: "x", 1: "x", 2: 1, 3: "x", 4: "x"},
    {-3: -2, -2: "x", -1: "x", 0: "x", 1: "x", 2: 1, 3: "x", 4: 3},
)
SCATTER_TO = (
    {-3: "x", -2: "x", -1: -2, 0: "x", 1: 0, 2: "x", 3: 2, 4: 3},
    {-3: -2, -2: "x", -1: "x", 0: "x", 1: "x", 2: 1, 3: "x", 4: "x"},
    {-3: -2, -2: -1, -1: "x", 0: "x", 1: "x", 2: 3, 3: "x", 4: 3},
    {-3: "x", -2: "x", -1: 0, 0: "x", 1: 0, 2: 1, 3: "x", 4: "x"},
)
GATHER_ORDER = (
    (0, "o", 1), (1, "o", 1), (3, "o", 1), (0, "t", 0), (2, "o", 1), (2, "o", -1), (1, "o", -1), (1, "t", 0),
    (2, "t", 0), (0, "o", -1), (3, "o", -1), (0, "t", 1), (0, "o", 2), (1, "o", 2), (3, "o", 2), (2, "o", 2),
    (3, "t", 1), (2, "t", 1), (2, "t", -1), (2, "o", -2), (1, "o", -2), (0, "t", -1), (0, "o", 3),
    (1, "t", -1), (3, "t", -1), (1, "o", 3), (3, "o", -2), (2, "o", 3), (3, "o", 3), (0, "o", -2),
    (0, "o", 4), (0, "t", 3), (2, "t", -2), (2, "o", -3), (0, "t", -2), (0, "t", 2), (1, "t", 3),
    (2, "o", 4), (1, "o", 4), (3, "t", 3), (2, "t", 3), (1, "o", -3), (3, "t", -2), (1, "t", -2),
    (0, "o", -3), (0, "t", -3), (2, "t", 4), (0, "t", 4), (1, "t", 2), (2, "t", -3), (2, "t", 2),
    (1, "t", 4), (3, "o", -3), (3, "o", 4), (3, "t", 0), (1, "t", 1), (3, "t", 4), (1, "t", -3),
    (3, "t", -3), (3, "t", 2), (0, "P", 0), (2, "P", 0), (1, "P", 0), (3, "P", 0),
)
SCATTER_ORDER = (
    (1, "M", 0), (1, "t", -3), (1, "t", 4), (2, "M", 0), (2, "t", 2), (1, "t", 3), (2, "t", 4), (2, "o", 4),
    (3, "M", 0), (3, "t", 4), (2, "t", -3), (0, "M", 0), (0, "t", 4), (3, "t", 2), (1, "o", -3),
    (0, "t", -1), (0, "t", -3), (3, "t", -3), (2, "o", -3), (0, "o", 4), (1, "o", 4), (2, "t", 3),
    (2, "t", -2), (3, "t", 3), (3, "o", 4), (0, "t", 3), (3, "t", -2), (0, "o", -3), (1, "t", 2),
    (3, "t", -1), (1, "t", -2), (0, "t", -2), (1, "o", 3), (2, "o", 3), (3, "o", -3), (0, "o", 3),
    (3, "o", 3), (0, "t", 2), (1, "t", -1), (3, "t", 1), (2, "t", 1), (1, "o", -2), (0, "t", 1), (1, "t", 1),
    (2, "t", -1), (1, "o", 2), (2, "o", 2), (2, "o", -2), (3, "o", 2), (3, "o", -2), (1, "t", 0),
    (2, "t", 0), (0, "o", -2), (0, "o", 2), (1, "o", 1), (1, "o", -1), (3, "t", 0), (2, "o", 1),
    (2, "o", -1), (0, "t", 0), (3, "o", 1), (3, "o", -1), (0, "o", -1), (0, "o", 1), (1, "F", 0),
    (2, "F", 0), (3, "F", 0), (0, "F", 0),
)
SLOT = {("o", p): i for i, p in enumerate(STEPS)} | {("t", p): 7 + i for i, p in enumerate((0,) + STEPS)}
SLOTS = 15


def kernel(
    sizes,
    tokens_hbm, gain_hbm, win_hbm, taps_hbm, res_hbm, rate_hbm, skip_hbm, wout_hbm,
    out,
    tok, gain, win, taps, res, rate, skip, wout,
    xg, proj, sig, gate, dec, res3, far, step3, ends, message, messages, rows32, before, heads, decays, inc,
    gated32, gated, part, land,
    load_sem, ag_send, ag_recv, rs_send, rs_recv, st_send, st_recv,
):
    ring, n_ctx, rows, width = sizes
    block_rows = 2 * ring * rows
    cols = width // SLICES
    seg = block_rows // SEGMENTS
    channels = rate.shape[1]

    dp, ctx, tensor = lax.axis_index("dp"), lax.axis_index("ctx"), lax.axis_index("tensor")
    plane, z = tensor // ring, tensor % ring

    def at(ctx_now, plane_now, z_now):
        return (dp, ctx_now, plane_now * ring + z_now)

    partner = at(ctx, 1 - plane, z)

    loads = [
        pltpu.make_async_copy(source, target, load_sem.at[i])
        for i, (source, target) in enumerate(
            (
                (tokens_hbm, tok), (gain_hbm, gain), (rate_hbm, rate), (res_hbm, res),
                (taps_hbm, taps), (skip_hbm, skip), (win_hbm, win), (wout_hbm, wout),
            )
        )
    ]
    for load in loads:
        load.start()

    barrier = pltpu.get_barrier_semaphore()
    peers = [partner, at(ctx, plane, (z + 1) % ring), at(ctx, plane, (z + ring - 1) % ring)]
    peers += [at((ctx + o) % n_ctx, plane, z) for o in range(1, n_ctx)]
    for peer in peers:
        pl.semaphore_signal(barrier, inc=1, device_id=peer, device_id_type=MESH)

    def ring_at(k, steps):
        return (z + (1 - 2 * (k % 2)) * steps + 2 * ring) % ring

    def where(kind, k, position):
        return (plane if kind == "o" else 1 - plane), ring_at(k, -position)

    def block(plane_now, z_now):
        return pl.ds(pl.multiple_of((plane_now * ring + z_now) * rows, rows), rows)

    def gather_copy(k, kind, position, source_kind, source, target):
        mine = xg.at[k, block(*where(source_kind, k, source)), :]
        slot = SLOT[kind, position]
        return pltpu.make_async_remote_copy(
            src_ref=mine, dst_ref=mine, send_sem=ag_send.at[k, slot], recv_sem=ag_recv.at[k, slot],
            device_id=target, device_id_type=MESH,
        )

    def scatter_copy(k, kind, position, target):
        slot = SLOT[kind, position]
        return pltpu.make_async_remote_copy(
            src_ref=part.at[k, block(*where(kind, k, position)), :], dst_ref=land.at[k, slot],
            send_sem=rs_send.at[k, slot], recv_sem=rs_recv.at[k, slot],
            device_id=target, device_id_type=MESH,
        )

    def toward(position):
        return position - 1 if position > 0 else position + 1

    loads[0].wait()
    loads[1].wait()
    values = tok[...].astype(jnp.float32)
    spread = jnp.mean(values * values, axis=-1, keepdims=True)
    normed = (values * lax.rsqrt(spread + EPSILON) * gain[...]).astype(jnp.bfloat16)
    for k in range(SLICES):
        xg[k, block(plane, z), :] = normed[:, k * cols : (k + 1) * cols]
    pl.semaphore_wait(barrier, len(peers))

    got = set()

    def need(k, kind, position):
        if (k, kind, position) not in got:
            got.add((k, kind, position))
            gather_copy(k, kind, position, kind, position, partner).wait_recv()

    def send_gather(k, kind, position):
        if kind == "o":
            source = toward(position)
            if source:
                need(k, "o", source)
            gather_copy(k, "o", position, "o", source, at(ctx, plane, ring_at(k, position - source))).start()
        elif GATHER_FROM[k][position] == "x":
            if position:
                need(k, "o", position)
            gather_copy(k, "t", position, "o", position, partner).start()
        else:
            source = GATHER_FROM[k][position]
            need(k, "t", source)
            gather_copy(k, "t", position, "t", source, at(ctx, plane, ring_at(k, position - source))).start()

    first_wait = next(i for i, (k, kind, p) in enumerate(GATHER_ORDER) if (kind, p) not in (("o", 1), ("o", -1), ("t", 0)))
    for step in GATHER_ORDER[:first_wait]:
        send_gather(*step)

    loads[2].wait()
    loads[3].wait()
    loads[4].wait()
    loads[5].wait()
    modes = rate.shape[0]
    for m in range(modes):
        step3[m] = jnp.broadcast_to(rate[m : m + 1, :], (SEGMENTS, channels))
        res3[m] = jnp.broadcast_to(res[m : m + 1, :], (SEGMENTS, channels))
    dec[...] = jnp.exp(-step3[...])
    far[...] = jnp.exp(step3[...] * (-float(seg)))
    segment = lax.broadcasted_iota(jnp.int32, (modes, SEGMENTS, channels), 1)
    step3[...] = jnp.exp(step3[...] * (segment.astype(jnp.float32) * (-float(seg))))
    decays[0] = jnp.exp(-rate[...])
    decays[1] = jnp.exp(rate[...] * (-float(block_rows)))
    decays[2] = jnp.exp(rate[...] * (-float(block_rows - 2)))
    decays[3] = jnp.exp(rate[...])

    def project(k):
        for p in STEPS:
            need(k, "o", p)
        for p in (0,) + STEPS:
            need(k, "t", p)
        for g in range(3):
            group = pl.ds(g * channels, channels)
            product = jnp.dot(xg[k], win[g, k * cols : (k + 1) * cols, :], preferred_element_type=jnp.float32)
            product = product.reshape(SEGMENTS, seg, channels)
            if len(projected) == 0:
                proj[:, :, group] = product
            else:
                proj[:, :, group] += product
        projected.append(k)

    projected = []
    for k, kind, position in GATHER_ORDER[first_wait:]:
        if kind == "P":
            if not projected:
                loads[6].wait()
            project(k)
        else:
            send_gather(k, kind, position)

    taps32 = taps[...].astype(jnp.float32)

    def tap(j, g):
        return taps32[j, g : g + 1, :]

    def short_mix(i, now, one, two):
        featured = []
        for g in range(3):
            group = slice(g * channels, (g + 1) * channels)
            featured.append(tap(0, g) * now[:, group] + tap(1, g) * one[:, group] + tap(2, g) * two[:, group])
        sig[i] = featured[0] * featured[2]
        gate[i] = featured[1]

    def short_step(i, carry):
        short_mix(i, proj[:, i, :], proj[:, i - 1, :], proj[:, i - 2, :])
        return carry

    lax.fori_loop(2, seg, short_step, 0, unroll=6)

    first_row = lax.broadcasted_iota(jnp.int32, (SEGMENTS, 3 * channels), 0) == 0
    first_sig = lax.broadcasted_iota(jnp.int32, (SEGMENTS, channels), 0) == 0
    row_zero, row_next = proj[:, 0, :], proj[:, 1, :]
    row_one = pltpu.roll(proj[:, seg - 1, :], 1, 0)
    row_two = pltpu.roll(proj[:, seg - 2, :], 1, 0)
    short_mix(0, row_zero, row_one, row_two)
    short_mix(1, row_next, row_zero, row_one)
    sig[0] = jnp.where(first_sig, 0.0, sig[0])
    sig[1] = jnp.where(first_sig, 0.0, sig[1])

    halves = [pl.ds(first, 128) for first in range(0, channels, 128)]
    lane = lax.broadcasted_iota(jnp.int32, (modes, SEGMENTS, 128), 1)
    for half in halves:

        def end_step(i, carry, half=half):
            return dec[:, :, half] * carry + sig[i, :, half][None]

        total = lax.fori_loop(0, seg, end_step, jnp.zeros((modes, SEGMENTS, 128), jnp.float32), unroll=8)
        leap = far[:, :, half]
        for hop in (1, 2, 4):
            total = total + jnp.where(lane >= hop, leap * pltpu.roll(total, hop, 1), 0.0)
            leap = leap * leap
        ends[:, :, half] = total

    message[0:modes, :] = ends[:, SEGMENTS - 1, :].astype(jnp.bfloat16)
    last = [proj[SEGMENTS - 1, seg - 2 : seg - 1, :], proj[SEGMENTS - 1, seg - 1 : seg, :]]
    outer = [row_zero[0:1, :], row_next[0:1, :]] + last
    rows32[...] = jnp.zeros(rows32.shape, jnp.float32)
    for r, row in enumerate(outer):
        rows32[r : r + 1, :] = row[:, 0:channels]
        rows32[4 + r : 5 + r, :] = row[:, 2 * channels :]
    for r, row in enumerate(last):
        rows32[8 + r : 9 + r, :] = row[:, channels : 2 * channels]
    message[modes:, :] = rows32[...].astype(jnp.bfloat16)
    copies = [
        pltpu.make_async_remote_copy(
            src_ref=message, dst_ref=messages.at[o - 1], send_sem=st_send.at[o - 1], recv_sem=st_recv.at[o - 1],
            device_id=at((ctx + o) % n_ctx, plane, z), device_id_type=MESH,
        )
        for o in range(1, n_ctx)
    ]
    for copy in copies:
        copy.start()

    for half in halves:
        ends[:, :, half] = jnp.where(lane >= 1, pltpu.roll(ends[:, :, half], 1, 1), 0.0)

    for k in range(SLICES):
        for kind, position in SLOT:
            gather_copy(k, kind, position, kind, position, partner).wait_send()

    for o in range(1, n_ctx):
        copies[o - 1].wait_recv()
        before[o - 1] = jnp.where(o <= ctx, messages[o - 1, modes:, :].astype(jnp.float32), 0.0)
    before[n_ctx - 1] = jnp.zeros(before.shape[1:], jnp.float32)
    before[n_ctx] = jnp.zeros(before.shape[1:], jnp.float32)

    def first_two(r, g):
        start, then = before[0:n_ctx, r, :], before[0:n_ctx, r + 1, :]
        two, one = before[1 : n_ctx + 1, r + 2, :], before[1 : n_ctx + 1, r + 3, :]
        return (
            tap(0, g) * start + tap(1, g) * one + tap(2, g) * two,
            tap(0, g) * then + tap(1, g) * start + tap(2, g) * one,
        )

    left, right = first_two(0, 0), first_two(4, 2)
    heads[0] = left[0] * right[0]
    heads[1] = left[1] * right[1]
    decay = decays[0]
    incoming = jnp.zeros(rate.shape, jnp.float32)
    for o in range(n_ctx - 1, 0, -1):
        ended = jnp.where(o <= ctx, messages[o - 1, 0:modes, :].astype(jnp.float32), 0.0)
        head = decay * heads[0, o - 1 : o, :] + heads[1, o - 1 : o, :]
        incoming = decays[1] * incoming + (ended + decays[2] * head)

    def halo(r):
        row = jnp.concatenate([before[0, r : r + 1, :], before[0, 8 + r - 2 : 9 + r - 2, :], before[0, 4 + r : 5 + r, :]], axis=1)
        return jnp.broadcast_to(row, (SEGMENTS, 3 * channels))

    row_one = jnp.where(first_row, halo(3), pltpu.roll(proj[:, seg - 1, :], 1, 0))
    row_two = jnp.where(first_row, halo(2), pltpu.roll(proj[:, seg - 2, :], 1, 0))
    row_zero = proj[:, 0, :]
    short_mix(0, row_zero, row_one, row_two)
    short_mix(1, proj[:, 1, :], row_zero, row_one)
    inc[0] = incoming
    inc[1] = incoming + decays[3] * (sig[0, 0:1, :] + decays[3] * sig[1, 0:1, :])
    first_sig = lax.broadcasted_iota(jnp.int32, (SEGMENTS, channels), 0) == 0
    for m in range(modes):
        ends[m] = ends[m] + step3[m] * jnp.where(first_sig, inc[0, m : m + 1, :], inc[1, m : m + 1, :])

    for half in halves:

        def long_step(i, carry, half=half):
            now = sig[i, :, half]
            carry = dec[:, :, half] * carry + now[None]
            mixed = jnp.sum(res3[:, :, half] * carry, axis=0)
            gated32[i, :, half] = gate[i, :, half] * (mixed + skip[:, half] * now)
            return carry

        lax.fori_loop(0, seg, long_step, ends[:, :, half], unroll=4)
    for s in range(SEGMENTS):
        gated[s * seg : (s + 1) * seg, :] = gated32[:, s, :].astype(jnp.bfloat16)

    loads[7].wait()

    def add(k, kind, position, terms):
        for term in terms:
            scatter_copy(k, *term, partner).wait_recv()
        mine = block(*where(kind, k, position))
        total = part[k, mine, :].astype(jnp.float32)
        for term in terms:
            total = total + land[k, SLOT[term]].astype(jnp.float32)
        return mine, total

    def terms_of(k, kind, position):
        terms = [("t", p) for p in STEPS if kind == "t" and SCATTER_TO[k][p] == position]
        if kind == "o":
            terms += [("o", p) for p in STEPS if toward(p) == position]
            terms += [("t", position)] if SCATTER_TO[k][position] == "x" else []
        return terms

    def send_scatter(k, kind, position):
        terms = terms_of(k, kind, position)
        if terms:
            mine, total = add(k, kind, position, terms)
            part[k, mine, :] = total.astype(jnp.bfloat16)
        target = toward(position) if kind == "o" else SCATTER_TO[k][position]
        device = partner if target == "x" else at(ctx, plane, ring_at(k, target - position))
        scatter_copy(k, kind, position, device).start()

    late = (("t", 0), ("o", 1), ("o", -1))

    def drain(k, kinds):
        for kind, position in kinds:
            scatter_copy(k, kind, position, partner).wait_send()

    finished = []
    for k, kind, position in SCATTER_ORDER:
        columns = slice(k * cols, (k + 1) * cols)
        if kind == "M":
            product = jnp.dot(gated[...], wout[:, columns], preferred_element_type=jnp.float32)
            part[k] = product.astype(jnp.bfloat16)
        elif kind == "F":
            drain(k, [other for other in SLOT if other not in late])
            _, total = add(k, "o", 0, terms_of(k, "o", 0))
            out[:, columns] = (total + tok[:, columns].astype(jnp.float32)).astype(jnp.bfloat16)
        else:
            send_scatter(k, kind, position)
    for k in range(SLICES):
        drain(k, late)
    for copy in copies:
        copy.wait_send()


def on_device(ring, n_ctx, tokens, norm_gain, in_weight, short_filter, residues, decay_rate, skip_gain, out_weight):
    rows, width = tokens.shape
    modes, channels = decay_rate.shape
    block_rows = 2 * ring * rows
    seg = block_rows // SEGMENTS
    cols = width // SLICES
    f32, bf16 = jnp.float32, jnp.bfloat16
    any_spec = pl.BlockSpec(memory_space=pl.ANY)
    table = pltpu.VMEM((modes, SEGMENTS, channels), f32)
    dma = pltpu.SemaphoreType.DMA
    return pl.pallas_call(
        functools.partial(kernel, (ring, n_ctx, rows, width)),
        out_shape=pltpu.VMEM((rows, width), bf16),
        in_specs=[any_spec] * 8,
        out_specs=pl.BlockSpec(memory_space=pltpu.VMEM),
        scratch_shapes=[
            pltpu.VMEM((rows, width), bf16),
            pltpu.VMEM((1, width), f32),
            pltpu.VMEM((3, width, channels), bf16),
            pltpu.VMEM(short_filter.shape, bf16),
            pltpu.VMEM((modes, channels), f32),
            pltpu.VMEM((modes, channels), f32),
            pltpu.VMEM((1, channels), f32),
            pltpu.VMEM((channels, width), bf16),
            pltpu.VMEM((SLICES, block_rows, cols), bf16),
            pltpu.VMEM((SEGMENTS, seg, 3 * channels), f32),
            pltpu.VMEM((seg, SEGMENTS, channels), f32),
            pltpu.VMEM((seg, SEGMENTS, channels), f32),
            table, table, table, table, table,
            pltpu.VMEM((modes + 16, channels), bf16),
            pltpu.VMEM((n_ctx - 1, modes + 16, channels), bf16),
            pltpu.VMEM((16, channels), f32),
            pltpu.VMEM((n_ctx + 1, 16, channels), f32),
            pltpu.VMEM((2, n_ctx, channels), f32),
            pltpu.VMEM((4, modes, channels), f32),
            pltpu.VMEM((2, modes, channels), f32),
            pltpu.VMEM((seg, SEGMENTS, channels), f32),
            pltpu.VMEM((block_rows, channels), bf16),
            pltpu.VMEM((SLICES, block_rows, cols), bf16),
            pltpu.VMEM((SLICES, SLOTS, rows, cols), bf16),
            dma((8,)),
            dma((SLICES, SLOTS)), dma((SLICES, SLOTS)),
            dma((SLICES, SLOTS)), dma((SLICES, SLOTS)),
            dma((n_ctx - 1,)), dma((n_ctx - 1,)),
        ],
        name="hyena_layer",
        cost_estimate=pl.CostEstimate(
            flops=2 * block_rows * width * channels * 4, bytes_accessed=8 * width * channels, transcendentals=0
        ),
        compiler_params=pltpu.CompilerParams(
            collective_id=0, has_side_effects=True, vmem_limit_bytes=60 * 2**20
        ),
    )(
        tokens, norm_gain.reshape(1, width), in_weight.transpose(1, 0, 2), short_filter,
        residues, decay_rate, skip_gain.reshape(1, channels), out_weight,
    )


def solution(mesh):
    ring, n_ctx = mesh.shape["tensor"] // 2, mesh.shape["ctx"]
    in_specs = (
        P(("dp", "ctx", "tensor"), None),
        P(),
        P(None, None, "tensor"),
        P(None, None, "tensor"),
        P(None, "tensor"),
        P(None, "tensor"),
        P("tensor"),
        P("tensor", None),
    )
    out_specs = P(("dp", "ctx", "tensor"), None)
    return jax.shard_map(
        functools.partial(on_device, ring, n_ctx),
        mesh=mesh, in_specs=in_specs, out_specs=out_specs, check_vma=False,
    )
```

```python
import functools

import jax
import jax.numpy as jnp
from jax import lax
from jax.experimental import pallas as pl
from jax.experimental.pallas import tpu as pltpu
from jax.sharding import PartitionSpec as P

EPSILON = 1e-06
MESH = pl.DeviceIdType.MESH
SLICES = 4
SEGMENTS = 8
STEPS = (1, 2, 3, 4, -1, -2, -3)
GATHER_FROM = (
    {-3: -2, -2: "x", -1: 0, 0: "x", 1: 2, 2: "x", 3: "x", 4: 3},
    {-3: -2, -2: -1, -1: 0, 0: "x", 1: "x", 2: "x", 3: "x", 4: "x"},
    {-3: "x", -2: "x", -1: 0, 0: "x", 1: 0, 2: 3, 3: "x", 4: 3},
    {-3: "x", -2: "x", -1: "x", 0: "x", 1: 2, 2: "x", 3: "x", 4: 3},
)
SCATTER_TO = (
    {-3: -2, -2: -1, -1: "x", 0: "x", 1: "x", 2: 1, 3: "x", 4: 3},
    {-3: "x", -2: -1, -1: "x", 0: "x", 1: 0, 2: "x", 3: "x", 4: "x"},
    {-3: -2, -2: "x", -1: "x", 0: "x", 1: "x", 2: "x", 3: "x", 4: 3},
    {-3: -2, -2: -1, -1: "x", 0: "x", 1: 0, 2: "x", 3: "x", 4: "x"},
)
GATHER_OWN = (
    {1: 0, 2: 0, 3: 2, 4: 3, -1: 0, -2: 0, -3: -2},
    {1: 0, 2: 1, 3: 2, 4: 2, -1: 0, -2: -1, -3: -2},
    {1: 0, 2: 0, 3: 2, 4: 3, -1: 0, -2: -1, -3: -2},
    {1: 0, 2: 0, 3: 2, 4: 3, -1: 0, -2: -1, -3: -2},
)
SCATTER_OWN = (
    {1: 0, 2: 1, 3: 1, 4: 3, -1: 0, -2: -1, -3: -2},
    {1: 0, 2: 0, 3: 2, 4: 3, -1: 0, -2: -1, -3: -2},
    {1: 0, 2: 0, 3: 2, 4: 3, -1: 0, -2: 0, -3: -2},
    {1: 0, 2: 0, 3: 2, 4: 3, -1: 0, -2: -1, -3: -2},
)
GATHER_ORDER = (
    (3, "o", -1), (3, "o", 2), (2, "o", 2), (2, "t", 0), (0, "o", 2), (1, "t", 0), (1, "o", -1), (1, "o", 1),
    (3, "t", 0), (2, "o", -1), (0, "o", -2), (3, "t", -1), (3, "t", 2), (0, "t", 0), (3, "o", -2),
    (3, "o", 3), (1, "t", 1), (2, "o", 3), (1, "t", -1), (1, "o", 2), (2, "o", -2), (0, "o", 3), (3, "o", 1),
    (0, "t", 2), (3, "o", -3), (2, "t", 1), (2, "t", -1), (0, "t", -2), (1, "o", -2), (3, "t", 3),
    (1, "o", 4), (1, "t", 2), (2, "o", -3), (1, "o", 3), (0, "o", 1), (1, "t", -2), (2, "t", 3), (0, "t", 3),
    (1, "o", -3), (3, "t", -2), (3, "t", -3), (3, "t", 4), (1, "t", 4), (3, "t", 1), (3, "o", 4),
    (1, "t", -3), (2, "t", 2), (0, "o", -1), (0, "t", -1), (0, "o", -3), (1, "t", 3), (2, "t", -2),
    (2, "o", 1), (2, "t", -3), (2, "o", 4), (2, "t", 4), (0, "t", 1), (0, "o", 4), (0, "t", 4), (0, "t", -3),
    (3, "P", 0), (1, "P", 0), (2, "P", 0), (0, "P", 0),
)
SCATTER_ORDER = (
    (2, "M", 0), (2, "t", -1), (2, "o", 4), (2, "t", 4), (2, "t", -3), (1, "M", 0), (1, "t", 4), (3, "M", 0),
    (3, "o", 1), (3, "t", 4), (2, "o", -3), (2, "t", 2), (3, "t", -3), (0, "M", 0), (1, "t", -3),
    (1, "t", -2), (0, "t", -3), (1, "t", 3), (3, "t", 3), (0, "t", 4), (0, "o", -3), (2, "o", -1),
    (3, "o", -3), (3, "t", -2), (1, "o", 4), (2, "t", 3), (3, "o", 4), (0, "o", 4), (0, "t", 3),
    (0, "t", -2), (0, "t", 2), (3, "t", 2), (3, "t", 1), (0, "o", -2), (1, "t", 2), (1, "o", -3),
    (3, "o", -2), (1, "o", 3), (0, "o", 2), (2, "t", 1), (3, "o", 3), (3, "t", -1), (1, "t", 1),
    (1, "t", -1), (2, "o", 3), (1, "o", 1), (2, "t", -2), (0, "t", 1), (1, "o", -2), (0, "o", 3),
    (0, "t", -1), (1, "o", 2), (3, "o", 2), (2, "o", 2), (3, "t", 0), (1, "t", 0), (3, "o", -1), (2, "t", 0),
    (0, "t", 0), (2, "o", 1), (2, "o", -2), (1, "o", -1), (0, "o", 1), (0, "o", -1), (1, "F", 0),
    (3, "F", 0), (2, "F", 0), (0, "F", 0),
)
SLOT = {("o", p): i for i, p in enumerate(STEPS)} | {("t", p): 7 + i for i, p in enumerate((0,) + STEPS)}
SLOTS = 15


def kernel(
    sizes,
    tokens_hbm, gain_hbm, win_hbm, taps_hbm, res_hbm, rate_hbm, skip_hbm, wout_hbm,
    out,
    tok, gain, win, taps, res, rate, skip, wout,
    xg, proj, sig, gate, dec, res3, far, step3, ends, message, messages, rows32, before, heads, decays, inc,
    gated32, gated, part, land,
    load_sem, ag_send, ag_recv, rs_send, rs_recv, st_send, st_recv,
):
    ring, n_ctx, rows, width = sizes
    block_rows = 2 * ring * rows
    cols = width // SLICES
    seg = block_rows // SEGMENTS
    channels = rate.shape[1]

    dp, ctx, tensor = lax.axis_index("dp"), lax.axis_index("ctx"), lax.axis_index("tensor")
    plane, z = tensor // ring, tensor % ring

    def at(ctx_now, plane_now, z_now):
        return (dp, ctx_now, plane_now * ring + z_now)

    partner = at(ctx, 1 - plane, z)

    loads = [
        pltpu.make_async_copy(source, target, load_sem.at[i])
        for i, (source, target) in enumerate(
            (
                (tokens_hbm, tok), (gain_hbm, gain), (rate_hbm, rate), (res_hbm, res),
                (taps_hbm, taps), (skip_hbm, skip), (win_hbm, win), (wout_hbm, wout),
            )
        )
    ]
    for load in loads:
        load.start()

    barrier = pltpu.get_barrier_semaphore()
    peers = [partner] + [at(ctx, plane, (z + steps) % ring) for steps in (1, 2, ring - 2, ring - 1)]
    peers += [at((ctx + o) % n_ctx, plane, z) for o in range(1, n_ctx)]
    for peer in peers:
        pl.semaphore_signal(barrier, inc=1, device_id=peer, device_id_type=MESH)

    def ring_at(k, steps):
        return (z + (1 - 2 * (k % 2)) * steps + 2 * ring) % ring

    def where(kind, k, position):
        return (plane if kind == "o" else 1 - plane), ring_at(k, -position)

    def block(plane_now, z_now):
        return pl.ds(pl.multiple_of((plane_now * ring + z_now) * rows, rows), rows)

    def gather_copy(k, kind, position, source_kind, source, target):
        mine = xg.at[k, block(*where(source_kind, k, source)), :]
        slot = SLOT[kind, position]
        return pltpu.make_async_remote_copy(
            src_ref=mine, dst_ref=mine, send_sem=ag_send.at[k, slot], recv_sem=ag_recv.at[k, slot],
            device_id=target, device_id_type=MESH,
        )

    def scatter_copy(k, kind, position, target):
        slot = SLOT[kind, position]
        return pltpu.make_async_remote_copy(
            src_ref=part.at[k, block(*where(kind, k, position)), :], dst_ref=land.at[k, slot],
            send_sem=rs_send.at[k, slot], recv_sem=rs_recv.at[k, slot],
            device_id=target, device_id_type=MESH,
        )

    loads[0].wait()
    loads[1].wait()
    values = tok[...].astype(jnp.float32)
    spread = jnp.mean(values * values, axis=-1, keepdims=True)
    normed = (values * lax.rsqrt(spread + EPSILON) * gain[...]).astype(jnp.bfloat16)
    for k in range(SLICES):
        xg[k, block(plane, z), :] = normed[:, k * cols : (k + 1) * cols]
    pl.semaphore_wait(barrier, len(peers))

    got = set()

    def need(k, kind, position):
        if (k, kind, position) not in got:
            got.add((k, kind, position))
            gather_copy(k, kind, position, kind, position, partner).wait_recv()

    def send_gather(k, kind, position):
        if kind == "o":
            source = GATHER_OWN[k][position]
            if source:
                need(k, "o", source)
            gather_copy(k, "o", position, "o", source, at(ctx, plane, ring_at(k, position - source))).start()
        elif GATHER_FROM[k][position] == "x":
            if position:
                need(k, "o", position)
            gather_copy(k, "t", position, "o", position, partner).start()
        else:
            source = GATHER_FROM[k][position]
            need(k, "t", source)
            gather_copy(k, "t", position, "t", source, at(ctx, plane, ring_at(k, position - source))).start()

    first_wait = next(i for i, (k, kind, p) in enumerate(GATHER_ORDER) if (kind, p) != ("t", 0) and (kind != "o" or GATHER_OWN[k][p]))
    for step in GATHER_ORDER[:first_wait]:
        send_gather(*step)

    loads[2].wait()
    loads[3].wait()
    loads[4].wait()
    loads[5].wait()
    modes = rate.shape[0]
    for m in range(modes):
        step3[m] = jnp.broadcast_to(rate[m : m + 1, :], (SEGMENTS, channels))
        res3[m] = jnp.broadcast_to(res[m : m + 1, :], (SEGMENTS, channels))
    dec[...] = jnp.exp(-step3[...])
    far[...] = jnp.exp(step3[...] * (-float(seg)))
    segment = lax.broadcasted_iota(jnp.int32, (modes, SEGMENTS, channels), 1)
    step3[...] = jnp.exp(step3[...] * (segment.astype(jnp.float32) * (-float(seg))))
    decays[0] = jnp.exp(-rate[...])
    decays[1] = jnp.exp(rate[...] * (-float(block_rows)))
    decays[2] = jnp.exp(rate[...] * (-float(block_rows - 2)))
    decays[3] = jnp.exp(rate[...])

    def project(k):
        for p in STEPS:
            need(k, "o", p)
        for p in (0,) + STEPS:
            need(k, "t", p)
        for g in range(3):
            group = pl.ds(g * channels, channels)
            product = jnp.dot(xg[k], win[g, k * cols : (k + 1) * cols, :], preferred_element_type=jnp.float32)
            product = product.reshape(SEGMENTS, seg, channels)
            if len(projected) == 0:
                proj[:, :, group] = product
            else:
                proj[:, :, group] += product
        projected.append(k)

    projected = []
    for k, kind, position in GATHER_ORDER[first_wait:]:
        if kind == "P":
            if not projected:
                loads[6].wait()
            project(k)
        else:
            send_gather(k, kind, position)

    taps32 = taps[...].astype(jnp.float32)

    def tap(j, g):
        return taps32[j, g : g + 1, :]

    def short_mix(i, now, one, two):
        featured = []
        for g in range(3):
            group = slice(g * channels, (g + 1) * channels)
            featured.append(tap(0, g) * now[:, group] + tap(1, g) * one[:, group] + tap(2, g) * two[:, group])
        sig[i] = featured[0] * featured[2]
        gate[i] = featured[1]

    def short_step(i, carry):
        short_mix(i, proj[:, i, :], proj[:, i - 1, :], proj[:, i - 2, :])
        return carry

    lax.fori_loop(2, seg, short_step, 0, unroll=6)

    first_row = lax.broadcasted_iota(jnp.int32, (SEGMENTS, 3 * channels), 0) == 0
    first_sig = lax.broadcasted_iota(jnp.int32, (SEGMENTS, channels), 0) == 0
    row_zero, row_next = proj[:, 0, :], proj[:, 1, :]
    row_one = pltpu.roll(proj[:, seg - 1, :], 1, 0)
    row_two = pltpu.roll(proj[:, seg - 2, :], 1, 0)
    short_mix(0, row_zero, row_one, row_two)
    short_mix(1, row_next, row_zero, row_one)
    sig[0] = jnp.where(first_sig, 0.0, sig[0])
    sig[1] = jnp.where(first_sig, 0.0, sig[1])

    halves = [pl.ds(first, 128) for first in range(0, channels, 128)]
    lane = lax.broadcasted_iota(jnp.int32, (modes, SEGMENTS, 128), 1)
    for half in halves:

        def end_step(i, carry, half=half):
            return dec[:, :, half] * carry + sig[i, :, half][None]

        total = lax.fori_loop(0, seg, end_step, jnp.zeros((modes, SEGMENTS, 128), jnp.float32), unroll=8)
        leap = far[:, :, half]
        for hop in (1, 2, 4):
            total = total + jnp.where(lane >= hop, leap * pltpu.roll(total, hop, 1), 0.0)
            leap = leap * leap
        ends[:, :, half] = total

    message[0:modes, :] = ends[:, SEGMENTS - 1, :].astype(jnp.bfloat16)
    last = [proj[SEGMENTS - 1, seg - 2 : seg - 1, :], proj[SEGMENTS - 1, seg - 1 : seg, :]]
    outer = [row_zero[0:1, :], row_next[0:1, :]] + last
    rows32[...] = jnp.zeros(rows32.shape, jnp.float32)
    for r, row in enumerate(outer):
        rows32[r : r + 1, :] = row[:, 0:channels]
        rows32[4 + r : 5 + r, :] = row[:, 2 * channels :]
    for r, row in enumerate(last):
        rows32[8 + r : 9 + r, :] = row[:, channels : 2 * channels]
    message[modes:, :] = rows32[...].astype(jnp.bfloat16)
    copies = [
        pltpu.make_async_remote_copy(
            src_ref=message, dst_ref=messages.at[o - 1], send_sem=st_send.at[o - 1], recv_sem=st_recv.at[o - 1],
            device_id=at((ctx + o) % n_ctx, plane, z), device_id_type=MESH,
        )
        for o in range(1, n_ctx)
    ]
    for copy in copies:
        copy.start()

    for half in halves:
        ends[:, :, half] = jnp.where(lane >= 1, pltpu.roll(ends[:, :, half], 1, 1), 0.0)

    for k in range(SLICES):
        for kind, position in SLOT:
            gather_copy(k, kind, position, kind, position, partner).wait_send()

    for o in range(1, n_ctx):
        copies[o - 1].wait_recv()
        before[o - 1] = jnp.where(o <= ctx, messages[o - 1, modes:, :].astype(jnp.float32), 0.0)
    before[n_ctx - 1] = jnp.zeros(before.shape[1:], jnp.float32)
    before[n_ctx] = jnp.zeros(before.shape[1:], jnp.float32)

    def first_two(r, g):
        start, then = before[0:n_ctx, r, :], before[0:n_ctx, r + 1, :]
        two, one = before[1 : n_ctx + 1, r + 2, :], before[1 : n_ctx + 1, r + 3, :]
        return (
            tap(0, g) * start + tap(1, g) * one + tap(2, g) * two,
            tap(0, g) * then + tap(1, g) * start + tap(2, g) * one,
        )

    left, right = first_two(0, 0), first_two(4, 2)
    heads[0] = left[0] * right[0]
    heads[1] = left[1] * right[1]
    decay = decays[0]
    incoming = jnp.zeros(rate.shape, jnp.float32)
    for o in range(n_ctx - 1, 0, -1):
        ended = jnp.where(o <= ctx, messages[o - 1, 0:modes, :].astype(jnp.float32), 0.0)
        head = decay * heads[0, o - 1 : o, :] + heads[1, o - 1 : o, :]
        incoming = decays[1] * incoming + (ended + decays[2] * head)

    def halo(r):
        row = jnp.concatenate([before[0, r : r + 1, :], before[0, 8 + r - 2 : 9 + r - 2, :], before[0, 4 + r : 5 + r, :]], axis=1)
        return jnp.broadcast_to(row, (SEGMENTS, 3 * channels))

    row_one = jnp.where(first_row, halo(3), pltpu.roll(proj[:, seg - 1, :], 1, 0))
    row_two = jnp.where(first_row, halo(2), pltpu.roll(proj[:, seg - 2, :], 1, 0))
    row_zero = proj[:, 0, :]
    short_mix(0, row_zero, row_one, row_two)
    short_mix(1, proj[:, 1, :], row_zero, row_one)
    inc[0] = incoming
    inc[1] = incoming + decays[3] * (sig[0, 0:1, :] + decays[3] * sig[1, 0:1, :])
    first_sig = lax.broadcasted_iota(jnp.int32, (SEGMENTS, channels), 0) == 0
    for m in range(modes):
        ends[m] = ends[m] + step3[m] * jnp.where(first_sig, inc[0, m : m + 1, :], inc[1, m : m + 1, :])

    for half in halves:

        def long_step(i, carry, half=half):
            now = sig[i, :, half]
            carry = dec[:, :, half] * carry + now[None]
            mixed = jnp.sum(res3[:, :, half] * carry, axis=0)
            gated32[i, :, half] = gate[i, :, half] * (mixed + skip[:, half] * now)
            return carry

        lax.fori_loop(0, seg, long_step, ends[:, :, half], unroll=4)
    for s in range(SEGMENTS):
        gated[s * seg : (s + 1) * seg, :] = gated32[:, s, :].astype(jnp.bfloat16)

    loads[7].wait()

    def add(k, kind, position, terms):
        for term in terms:
            scatter_copy(k, *term, partner).wait_recv()
        mine = block(*where(kind, k, position))
        total = part[k, mine, :].astype(jnp.float32)
        for term in terms:
            total = total + land[k, SLOT[term]].astype(jnp.float32)
        return mine, total

    def terms_of(k, kind, position):
        terms = [("t", p) for p in STEPS if kind == "t" and SCATTER_TO[k][p] == position]
        if kind == "o":
            terms += [("o", p) for p in STEPS if SCATTER_OWN[k][p] == position]
            terms += [("t", position)] if SCATTER_TO[k][position] == "x" else []
        return terms

    def send_scatter(k, kind, position):
        terms = terms_of(k, kind, position)
        if terms:
            mine, total = add(k, kind, position, terms)
            part[k, mine, :] = total.astype(jnp.bfloat16)
        target = (SCATTER_OWN if kind == "o" else SCATTER_TO)[k][position]
        device = partner if target == "x" else at(ctx, plane, ring_at(k, target - position))
        scatter_copy(k, kind, position, device).start()

    def drain(k, kinds):
        for kind, position in kinds:
            scatter_copy(k, kind, position, partner).wait_send()

    finished = []
    for k, kind, position in SCATTER_ORDER:
        columns = slice(k * cols, (k + 1) * cols)
        if kind == "M":
            product = jnp.dot(gated[...], wout[:, columns], preferred_element_type=jnp.float32)
            part[k] = product.astype(jnp.bfloat16)
        elif kind == "F":
            drain(k, [other for other in SLOT if other not in terms_of(k, "o", 0)])
            _, total = add(k, "o", 0, terms_of(k, "o", 0))
            out[:, columns] = (total + tok[:, columns].astype(jnp.float32)).astype(jnp.bfloat16)
        else:
            send_scatter(k, kind, position)
    for k in range(SLICES):
        drain(k, terms_of(k, "o", 0))
    for copy in copies:
        copy.wait_send()


def on_device(ring, n_ctx, tokens, norm_gain, in_weight, short_filter, residues, decay_rate, skip_gain, out_weight):
    rows, width = tokens.shape
    modes, channels = decay_rate.shape
    block_rows = 2 * ring * rows
    seg = block_rows // SEGMENTS
    cols = width // SLICES
    f32, bf16 = jnp.float32, jnp.bfloat16
    any_spec = pl.BlockSpec(memory_space=pl.ANY)
    table = pltpu.VMEM((modes, SEGMENTS, channels), f32)
    dma = pltpu.SemaphoreType.DMA
    return pl.pallas_call(
        functools.partial(kernel, (ring, n_ctx, rows, width)),
        out_shape=pltpu.VMEM((rows, width), bf16),
        in_specs=[any_spec] * 8,
        out_specs=pl.BlockSpec(memory_space=pltpu.VMEM),
        scratch_shapes=[
            pltpu.VMEM((rows, width), bf16),
            pltpu.VMEM((1, width), f32),
            pltpu.VMEM((3, width, channels), bf16),
            pltpu.VMEM(short_filter.shape, bf16),
            pltpu.VMEM((modes, channels), f32),
            pltpu.VMEM((modes, channels), f32),
            pltpu.VMEM((1, channels), f32),
            pltpu.VMEM((channels, width), bf16),
            pltpu.VMEM((SLICES, block_rows, cols), bf16),
            pltpu.VMEM((SEGMENTS, seg, 3 * channels), f32),
            pltpu.VMEM((seg, SEGMENTS, channels), f32),
            pltpu.VMEM((seg, SEGMENTS, channels), f32),
            table, table, table, table, table,
            pltpu.VMEM((modes + 16, channels), bf16),
            pltpu.VMEM((n_ctx - 1, modes + 16, channels), bf16),
            pltpu.VMEM((16, channels), f32),
            pltpu.VMEM((n_ctx + 1, 16, channels), f32),
            pltpu.VMEM((2, n_ctx, channels), f32),
            pltpu.VMEM((4, modes, channels), f32),
            pltpu.VMEM((2, modes, channels), f32),
            pltpu.VMEM((seg, SEGMENTS, channels), f32),
            pltpu.VMEM((block_rows, channels), bf16),
            pltpu.VMEM((SLICES, block_rows, cols), bf16),
            pltpu.VMEM((SLICES, SLOTS, rows, cols), bf16),
            dma((8,)),
            dma((SLICES, SLOTS)), dma((SLICES, SLOTS)),
            dma((SLICES, SLOTS)), dma((SLICES, SLOTS)),
            dma((n_ctx - 1,)), dma((n_ctx - 1,)),
        ],
        name="hyena_layer",
        cost_estimate=pl.CostEstimate(
            flops=2 * block_rows * width * channels * 4, bytes_accessed=8 * width * channels, transcendentals=0
        ),
        compiler_params=pltpu.CompilerParams(
            collective_id=0, has_side_effects=True, vmem_limit_bytes=60 * 2**20
        ),
    )(
        tokens, norm_gain.reshape(1, width), in_weight.transpose(1, 0, 2), short_filter,
        residues, decay_rate, skip_gain.reshape(1, channels), out_weight,
    )


def solution(mesh):
    ring, n_ctx = mesh.shape["tensor"] // 2, mesh.shape["ctx"]
    in_specs = (
        P(("dp", "ctx", "tensor"), None),
        P(),
        P(None, None, "tensor"),
        P(None, None, "tensor"),
        P(None, "tensor"),
        P(None, "tensor"),
        P("tensor"),
        P("tensor", None),
    )
    out_specs = P(("dp", "ctx", "tensor"), None)
    return jax.shard_map(
        functools.partial(on_device, ring, n_ctx),
        mesh=mesh, in_specs=in_specs, out_specs=out_specs, check_vma=False,
    )
```

```python
import functools

import jax
import jax.numpy as jnp
from jax import lax
from jax.experimental import pallas as pl
from jax.experimental.pallas import tpu as pltpu
from jax.sharding import PartitionSpec as P

EPSILON = 1e-06
MESH = pl.DeviceIdType.MESH
SLICES = 4
SEGMENTS = 8
STEPS = (1, 2, 3, 4, -1, -2, -3)
GATHER_FROM = (
    {-3: -2, -2: "x", -1: 0, 0: "x", 1: 2, 2: "x", 3: "x", 4: 3},
    {-3: -2, -2: -1, -1: 0, 0: "x", 1: "x", 2: "x", 3: "x", 4: "x"},
    {-3: "x", -2: "x", -1: 0, 0: "x", 1: 0, 2: 3, 3: "x", 4: 3},
    {-3: "x", -2: "x", -1: "x", 0: "x", 1: 2, 2: "x", 3: "x", 4: 3},
)
SCATTER_TO = (
    {-3: -2, -2: -1, -1: "x", 0: "x", 1: "x", 2: 1, 3: "x", 4: 3},
    {-3: "x", -2: -1, -1: "x", 0: "x", 1: 0, 2: "x", 3: "x", 4: "x"},
    {-3: -2, -2: "x", -1: "x", 0: "x", 1: "x", 2: "x", 3: "x", 4: 3},
    {-3: -2, -2: -1, -1: "x", 0: "x", 1: 0, 2: "x", 3: "x", 4: "x"},
)
GATHER_OWN = (
    {1: 0, 2: 0, 3: 2, 4: 3, -1: 0, -2: 0, -3: -2},
    {1: 0, 2: 1, 3: 2, 4: 2, -1: 0, -2: -1, -3: -2},
    {1: 0, 2: 0, 3: 2, 4: 3, -1: 0, -2: -1, -3: -2},
    {1: 0, 2: 0, 3: 2, 4: 3, -1: 0, -2: -1, -3: -2},
)
SCATTER_OWN = (
    {1: 0, 2: 1, 3: 1, 4: 3, -1: 0, -2: -1, -3: -2},
    {1: 0, 2: 0, 3: 2, 4: 3, -1: 0, -2: -1, -3: -2},
    {1: 0, 2: 0, 3: 2, 4: 3, -1: 0, -2: 0, -3: -2},
    {1: 0, 2: 0, 3: 2, 4: 3, -1: 0, -2: -1, -3: -2},
)
GATHER_ORDER = (
    (3, "o", -1), (3, "o", 2), (2, "o", 2), (2, "t", 0), (0, "o", 2), (1, "t", 0), (1, "o", -1), (1, "o", 1),
    (3, "t", 0), (2, "o", -1), (0, "o", -2), (3, "t", -1), (3, "t", 2), (0, "t", 0), (3, "o", -2),
    (3, "o", 3), (1, "t", 1), (2, "o", 3), (1, "t", -1), (1, "o", 2), (2, "o", -2), (0, "o", 3), (3, "o", 1),
    (0, "t", 2), (3, "o", -3), (2, "t", 1), (2, "t", -1), (0, "t", -2), (1, "o", -2), (3, "t", 3),
    (1, "o", 4), (1, "t", 2), (2, "o", -3), (1, "o", 3), (0, "o", 1), (1, "t", -2), (2, "t", 3), (0, "t", 3),
    (1, "o", -3), (3, "t", -2), (3, "t", -3), (3, "t", 4), (1, "t", 4), (3, "t", 1), (3, "o", 4),
    (1, "t", -3), (2, "t", 2), (0, "o", -1), (0, "t", -1), (0, "o", -3), (1, "t", 3), (2, "t", -2),
    (2, "o", 1), (2, "t", -3), (2, "o", 4), (2, "t", 4), (0, "t", 1), (0, "o", 4), (0, "t", 4), (0, "t", -3),
    (3, "P", 0), (1, "P", 0), (2, "P", 0), (0, "P", 0),
)
SCATTER_ORDER = (
    (2, "M", 0), (2, "t", -1), (2, "o", 4), (2, "t", 4), (2, "t", -3), (1, "M", 0), (1, "t", 4), (3, "M", 0),
    (3, "o", 1), (3, "t", 4), (2, "o", -3), (2, "t", 2), (3, "t", -3), (0, "M", 0), (1, "t", -3),
    (1, "t", -2), (0, "t", -3), (1, "t", 3), (3, "t", 3), (0, "t", 4), (0, "o", -3), (2, "o", -1),
    (3, "o", -3), (3, "t", -2), (1, "o", 4), (2, "t", 3), (3, "o", 4), (0, "o", 4), (0, "t", 3),
    (0, "t", -2), (0, "t", 2), (3, "t", 2), (3, "t", 1), (0, "o", -2), (1, "t", 2), (1, "o", -3),
    (3, "o", -2), (1, "o", 3), (0, "o", 2), (2, "t", 1), (3, "o", 3), (3, "t", -1), (1, "t", 1),
    (1, "t", -1), (2, "o", 3), (1, "o", 1), (2, "t", -2), (0, "t", 1), (1, "o", -2), (0, "o", 3),
    (0, "t", -1), (1, "o", 2), (3, "o", 2), (2, "o", 2), (3, "t", 0), (1, "t", 0), (3, "o", -1), (2, "t", 0),
    (0, "t", 0), (2, "o", 1), (2, "o", -2), (1, "o", -1), (0, "o", 1), (0, "o", -1), (1, "F", 0),
    (3, "F", 0), (2, "F", 0), (0, "F", 0),
)
SLOT = {("o", p): i for i, p in enumerate(STEPS)} | {("t", p): 7 + i for i, p in enumerate((0,) + STEPS)}
SLOTS = 15


def kernel(
    sizes,
    tokens_hbm, gain_hbm, win_hbm, taps_hbm, res_hbm, rate_hbm, skip_hbm, wout_hbm,
    out,
    tok, gain, win, taps, res, rate, skip, wout,
    xg, proj, sig, gate, dec, res3, far, step3, ends, message, messages, rows32, before, heads, decays, inc,
    gated32, gated, part, land,
    load_sem, ag_send, ag_recv, rs_send, rs_recv, st_send, st_recv,
):
    ring, n_ctx, rows, width = sizes
    block_rows = 2 * ring * rows
    cols = width // SLICES
    seg = block_rows // SEGMENTS
    channels = rate.shape[1]

    dp, ctx, tensor = lax.axis_index("dp"), lax.axis_index("ctx"), lax.axis_index("tensor")
    plane, z = tensor // ring, tensor % ring

    def at(ctx_now, plane_now, z_now):
        return (dp, ctx_now, plane_now * ring + z_now)

    partner = at(ctx, 1 - plane, z)

    loads = [
        pltpu.make_async_copy(source, target, load_sem.at[i])
        for i, (source, target) in enumerate(
            (
                (tokens_hbm, tok), (gain_hbm, gain), (rate_hbm, rate), (res_hbm, res),
                (taps_hbm, taps), (skip_hbm, skip), (win_hbm, win), (wout_hbm, wout),
            )
        )
    ]
    for load in loads:
        load.start()

    messages[...] = jnp.zeros(messages.shape, messages.dtype)
    barrier = pltpu.get_barrier_semaphore()
    peers = [partner] + [at(ctx, plane, (z + steps) % ring) for steps in (1, 2, ring - 2, ring - 1)]
    peers += [at((ctx + o) % n_ctx, plane, z) for o in range(1, n_ctx)]
    for peer in peers:
        pl.semaphore_signal(barrier, inc=1, device_id=peer, device_id_type=MESH)

    def ring_at(k, steps):
        return (z + (1 - 2 * (k % 2)) * steps + 2 * ring) % ring

    def where(kind, k, position):
        return (plane if kind == "o" else 1 - plane), ring_at(k, -position)

    def block(plane_now, z_now):
        return pl.ds(pl.multiple_of((plane_now * ring + z_now) * rows, rows), rows)

    def gather_copy(k, kind, position, source_kind, source, target):
        mine = xg.at[k, block(*where(source_kind, k, source)), :]
        slot = SLOT[kind, position]
        return pltpu.make_async_remote_copy(
            src_ref=mine, dst_ref=mine, send_sem=ag_send.at[k, slot], recv_sem=ag_recv.at[k, slot],
            device_id=target, device_id_type=MESH,
        )

    def scatter_copy(k, kind, position, target):
        slot = SLOT[kind, position]
        return pltpu.make_async_remote_copy(
            src_ref=part.at[k, block(*where(kind, k, position)), :], dst_ref=land.at[k, slot],
            send_sem=rs_send.at[k, slot], recv_sem=rs_recv.at[k, slot],
            device_id=target, device_id_type=MESH,
        )

    loads[0].wait()
    loads[1].wait()
    values = tok[...].astype(jnp.float32)
    spread = jnp.mean(values * values, axis=-1, keepdims=True)
    normed = (values * lax.rsqrt(spread + EPSILON) * gain[...]).astype(jnp.bfloat16)
    for k in range(SLICES):
        xg[k, block(plane, z), :] = normed[:, k * cols : (k + 1) * cols]
    pl.semaphore_wait(barrier, len(peers))

    got = set()

    def need(k, kind, position):
        if (k, kind, position) not in got:
            got.add((k, kind, position))
            gather_copy(k, kind, position, kind, position, partner).wait_recv()

    def send_gather(k, kind, position):
        if kind == "o":
            source = GATHER_OWN[k][position]
            if source:
                need(k, "o", source)
            gather_copy(k, "o", position, "o", source, at(ctx, plane, ring_at(k, position - source))).start()
        elif GATHER_FROM[k][position] == "x":
            if position:
                need(k, "o", position)
            gather_copy(k, "t", position, "o", position, partner).start()
        else:
            source = GATHER_FROM[k][position]
            need(k, "t", source)
            gather_copy(k, "t", position, "t", source, at(ctx, plane, ring_at(k, position - source))).start()

    first_wait = next(i for i, (k, kind, p) in enumerate(GATHER_ORDER) if (kind, p) != ("t", 0) and (kind != "o" or GATHER_OWN[k][p]))
    for step in GATHER_ORDER[:first_wait]:
        send_gather(*step)

    loads[2].wait()
    loads[3].wait()
    loads[4].wait()
    loads[5].wait()
    modes = rate.shape[0]
    for m in range(modes):
        step3[m] = jnp.broadcast_to(rate[m : m + 1, :], (SEGMENTS, channels))
        res3[m] = jnp.broadcast_to(res[m : m + 1, :], (SEGMENTS, channels))
    dec[...] = jnp.exp(-step3[...])
    far[...] = jnp.exp(step3[...] * (-float(seg)))
    segment = lax.broadcasted_iota(jnp.int32, (modes, SEGMENTS, channels), 1)
    step3[...] = jnp.exp(step3[...] * (segment.astype(jnp.float32) * (-float(seg))))
    decays[0] = jnp.exp(-rate[...])
    decays[1] = jnp.exp(rate[...] * (-float(block_rows)))
    decays[2] = jnp.exp(rate[...] * (-float(block_rows - 2)))
    decays[3] = jnp.exp(rate[...])

    def project(k):
        for p in STEPS:
            need(k, "o", p)
        for p in (0,) + STEPS:
            need(k, "t", p)
        for g in range(3):
            group = pl.ds(g * channels, channels)
            product = jnp.dot(xg[k], win[g, k * cols : (k + 1) * cols, :], preferred_element_type=jnp.float32)
            product = product.reshape(SEGMENTS, seg, channels)
            if len(projected) == 0:
                proj[:, :, group] = product
            else:
                proj[:, :, group] += product
        projected.append(k)

    projected = []
    for k, kind, position in GATHER_ORDER[first_wait:]:
        if kind == "P":
            if not projected:
                loads[6].wait()
            project(k)
        else:
            send_gather(k, kind, position)

    taps32 = taps[...].astype(jnp.float32)

    def tap(j, g):
        return taps32[j, g : g + 1, :]

    def short_mix(i, now, one, two):
        featured = []
        for g in range(3):
            group = slice(g * channels, (g + 1) * channels)
            featured.append(tap(0, g) * now[:, group] + tap(1, g) * one[:, group] + tap(2, g) * two[:, group])
        sig[i] = featured[0] * featured[2]
        gate[i] = featured[1]

    def short_step(i, carry):
        short_mix(i, proj[:, i, :], proj[:, i - 1, :], proj[:, i - 2, :])
        return carry

    lax.fori_loop(2, seg, short_step, 0, unroll=True)

    first_row = lax.broadcasted_iota(jnp.int32, (SEGMENTS, 3 * channels), 0) == 0
    first_sig = lax.broadcasted_iota(jnp.int32, (SEGMENTS, channels), 0) == 0
    row_zero, row_next = proj[:, 0, :], proj[:, 1, :]
    row_one = pltpu.roll(proj[:, seg - 1, :], 1, 0)
    row_two = pltpu.roll(proj[:, seg - 2, :], 1, 0)
    short_mix(0, row_zero, row_one, row_two)
    short_mix(1, row_next, row_zero, row_one)
    sig[0] = jnp.where(first_sig, 0.0, sig[0])
    sig[1] = jnp.where(first_sig, 0.0, sig[1])

    halves = [pl.ds(first, 128) for first in range(0, channels, 128)]
    lane = lax.broadcasted_iota(jnp.int32, (modes, SEGMENTS, 128), 1)
    for half in halves:

        def end_step(i, carry, half=half):
            return dec[:, :, half] * carry + sig[i, :, half][None]

        total = lax.fori_loop(0, seg, end_step, jnp.zeros((modes, SEGMENTS, 128), jnp.float32), unroll=True)
        leap = far[:, :, half]
        for hop in (1, 2, 4):
            total = total + jnp.where(lane >= hop, leap * pltpu.roll(total, hop, 1), 0.0)
            leap = leap * leap
        ends[:, :, half] = total

    message[0:modes, :] = ends[:, SEGMENTS - 1, :].astype(jnp.bfloat16)
    last = [proj[SEGMENTS - 1, seg - 2 : seg - 1, :], proj[SEGMENTS - 1, seg - 1 : seg, :]]
    outer = [row_zero[0:1, :], row_next[0:1, :]] + last
    rows32[...] = jnp.zeros(rows32.shape, jnp.float32)
    for r, row in enumerate(outer):
        rows32[r : r + 1, :] = row[:, 0:channels]
        rows32[4 + r : 5 + r, :] = row[:, 2 * channels :]
    for r, row in enumerate(last):
        rows32[8 + r : 9 + r, :] = row[:, channels : 2 * channels]
    message[modes:, :] = rows32[...].astype(jnp.bfloat16)
    copies = [
        pltpu.make_async_remote_copy(
            src_ref=message, dst_ref=messages.at[o - 1], send_sem=st_send.at[o - 1], recv_sem=st_recv.at[o - 1],
            device_id=at((ctx + o) % n_ctx, plane, z), device_id_type=MESH,
        )
        for o in range(1, n_ctx)
    ]
    for o, copy in enumerate(copies, 1):

        @pl.when(ctx + o < n_ctx)
        def _(copy=copy):
            copy.start()


    for half in halves:
        ends[:, :, half] = jnp.where(lane >= 1, pltpu.roll(ends[:, :, half], 1, 1), 0.0)

    for k in range(SLICES):
        for kind, position in SLOT:
            gather_copy(k, kind, position, kind, position, partner).wait_send()

    for o in range(1, n_ctx):

        @pl.when(o <= ctx)
        def _(o=o):
            copies[o - 1].wait_recv()

        before[o - 1] = messages[o - 1, modes:, :].astype(jnp.float32)
    before[n_ctx - 1] = jnp.zeros(before.shape[1:], jnp.float32)
    before[n_ctx] = jnp.zeros(before.shape[1:], jnp.float32)

    def first_two(r, g):
        start, then = before[0:n_ctx, r, :], before[0:n_ctx, r + 1, :]
        two, one = before[1 : n_ctx + 1, r + 2, :], before[1 : n_ctx + 1, r + 3, :]
        return (
            tap(0, g) * start + tap(1, g) * one + tap(2, g) * two,
            tap(0, g) * then + tap(1, g) * start + tap(2, g) * one,
        )

    left, right = first_two(0, 0), first_two(4, 2)
    heads[0] = left[0] * right[0]
    heads[1] = left[1] * right[1]
    decay = decays[0]
    incoming = jnp.zeros(rate.shape, jnp.float32)
    for o in range(n_ctx - 1, 0, -1):
        ended = messages[o - 1, 0:modes, :].astype(jnp.float32)
        head = decay * heads[0, o - 1 : o, :] + heads[1, o - 1 : o, :]
        incoming = decays[1] * incoming + (ended + decays[2] * head)

    def halo(r):
        row = jnp.concatenate([before[0, r : r + 1, :], before[0, 8 + r - 2 : 9 + r - 2, :], before[0, 4 + r : 5 + r, :]], axis=1)
        return jnp.broadcast_to(row, (SEGMENTS, 3 * channels))

    row_one = jnp.where(first_row, halo(3), pltpu.roll(proj[:, seg - 1, :], 1, 0))
    row_two = jnp.where(first_row, halo(2), pltpu.roll(proj[:, seg - 2, :], 1, 0))
    row_zero = proj[:, 0, :]
    short_mix(0, row_zero, row_one, row_two)
    short_mix(1, proj[:, 1, :], row_zero, row_one)
    inc[0] = incoming
    inc[1] = incoming + decays[3] * (sig[0, 0:1, :] + decays[3] * sig[1, 0:1, :])
    first_sig = lax.broadcasted_iota(jnp.int32, (SEGMENTS, channels), 0) == 0
    for m in range(modes):
        ends[m] = ends[m] + step3[m] * jnp.where(first_sig, inc[0, m : m + 1, :], inc[1, m : m + 1, :])

    for half in halves:

        def long_step(i, carry, half=half):
            now = sig[i, :, half]
            carry = dec[:, :, half] * carry + now[None]
            mixed = jnp.sum(res3[:, :, half] * carry, axis=0)
            gated32[i, :, half] = gate[i, :, half] * (mixed + skip[:, half] * now)
            return carry

        lax.fori_loop(0, seg, long_step, ends[:, :, half], unroll=True)
    for s in range(SEGMENTS):
        gated[s * seg : (s + 1) * seg, :] = gated32[:, s, :].astype(jnp.bfloat16)

    loads[7].wait()

    def add(k, kind, position, terms):
        for term in terms:
            scatter_copy(k, *term, partner).wait_recv()
        mine = block(*where(kind, k, position))
        total = part[k, mine, :].astype(jnp.float32)
        for term in terms:
            total = total + land[k, SLOT[term]].astype(jnp.float32)
        return mine, total

    def terms_of(k, kind, position):
        terms = [("t", p) for p in STEPS if kind == "t" and SCATTER_TO[k][p] == position]
        if kind == "o":
            terms += [("o", p) for p in STEPS if SCATTER_OWN[k][p] == position]
            terms += [("t", position)] if SCATTER_TO[k][position] == "x" else []
        return terms

    def send_scatter(k, kind, position):
        terms = terms_of(k, kind, position)
        if terms:
            mine, total = add(k, kind, position, terms)
            part[k, mine, :] = total.astype(jnp.bfloat16)
        target = (SCATTER_OWN if kind == "o" else SCATTER_TO)[k][position]
        device = partner if target == "x" else at(ctx, plane, ring_at(k, target - position))
        scatter_copy(k, kind, position, device).start()

    def drain(k, kinds):
        for kind, position in kinds:
            scatter_copy(k, kind, position, partner).wait_send()

    finished = []
    for k, kind, position in SCATTER_ORDER:
        columns = slice(k * cols, (k + 1) * cols)
        if kind == "M":
            product = jnp.dot(gated[...], wout[:, columns], preferred_element_type=jnp.float32)
            part[k] = product.astype(jnp.bfloat16)
        elif kind == "F":
            drain(k, [other for other in SLOT if other not in terms_of(k, "o", 0)])
            _, total = add(k, "o", 0, terms_of(k, "o", 0))
            out[:, columns] = (total + tok[:, columns].astype(jnp.float32)).astype(jnp.bfloat16)
        else:
            send_scatter(k, kind, position)
    for k in range(SLICES):
        drain(k, terms_of(k, "o", 0))
    for o, copy in enumerate(copies, 1):

        @pl.when(ctx + o < n_ctx)
        def _(copy=copy):
            copy.wait_send()


def on_device(ring, n_ctx, tokens, norm_gain, in_weight, short_filter, residues, decay_rate, skip_gain, out_weight):
    rows, width = tokens.shape
    modes, channels = decay_rate.shape
    block_rows = 2 * ring * rows
    seg = block_rows // SEGMENTS
    cols = width // SLICES
    f32, bf16 = jnp.float32, jnp.bfloat16
    any_spec = pl.BlockSpec(memory_space=pl.ANY)
    table = pltpu.VMEM((modes, SEGMENTS, channels), f32)
    dma = pltpu.SemaphoreType.DMA
    return pl.pallas_call(
        functools.partial(kernel, (ring, n_ctx, rows, width)),
        out_shape=pltpu.VMEM((rows, width), bf16),
        in_specs=[any_spec] * 8,
        out_specs=pl.BlockSpec(memory_space=pltpu.VMEM),
        scratch_shapes=[
            pltpu.VMEM((rows, width), bf16),
            pltpu.VMEM((1, width), f32),
            pltpu.VMEM((3, width, channels), bf16),
            pltpu.VMEM(short_filter.shape, bf16),
            pltpu.VMEM((modes, channels), f32),
            pltpu.VMEM((modes, channels), f32),
            pltpu.VMEM((1, channels), f32),
            pltpu.VMEM((channels, width), bf16),
            pltpu.VMEM((SLICES, block_rows, cols), bf16),
            pltpu.VMEM((SEGMENTS, seg, 3 * channels), f32),
            pltpu.VMEM((seg, SEGMENTS, channels), f32),
            pltpu.VMEM((seg, SEGMENTS, channels), f32),
            table, table, table, table, table,
            pltpu.VMEM((modes + 16, channels), bf16),
            pltpu.VMEM((n_ctx - 1, modes + 16, channels), bf16),
            pltpu.VMEM((16, channels), f32),
            pltpu.VMEM((n_ctx + 1, 16, channels), f32),
            pltpu.VMEM((2, n_ctx, channels), f32),
            pltpu.VMEM((4, modes, channels), f32),
            pltpu.VMEM((2, modes, channels), f32),
            pltpu.VMEM((seg, SEGMENTS, channels), f32),
            pltpu.VMEM((block_rows, channels), bf16),
            pltpu.VMEM((SLICES, block_rows, cols), bf16),
            pltpu.VMEM((SLICES, SLOTS, rows, cols), bf16),
            dma((8,)),
            dma((SLICES, SLOTS)), dma((SLICES, SLOTS)),
            dma((SLICES, SLOTS)), dma((SLICES, SLOTS)),
            dma((n_ctx - 1,)), dma((n_ctx - 1,)),
        ],
        name="hyena_layer",
        cost_estimate=pl.CostEstimate(
            flops=2 * block_rows * width * channels * 4, bytes_accessed=8 * width * channels, transcendentals=0
        ),
        compiler_params=pltpu.CompilerParams(
            collective_id=0, has_side_effects=True, vmem_limit_bytes=60 * 2**20
        ),
    )(
        tokens, norm_gain.reshape(1, width), in_weight.transpose(1, 0, 2), short_filter,
        residues, decay_rate, skip_gain.reshape(1, channels), out_weight,
    )


def solution(mesh):
    ring, n_ctx = mesh.shape["tensor"] // 2, mesh.shape["ctx"]
    in_specs = (
        P(("dp", "ctx", "tensor"), None),
        P(),
        P(None, None, "tensor"),
        P(None, None, "tensor"),
        P(None, "tensor"),
        P(None, "tensor"),
        P("tensor"),
        P("tensor", None),
    )
    out_specs = P(("dp", "ctx", "tensor"), None)
    return jax.shard_map(
        functools.partial(on_device, ring, n_ctx),
        mesh=mesh, in_specs=in_specs, out_specs=out_specs, check_vma=False,
    )
```

```python
import functools

import jax
import jax.numpy as jnp
from jax import lax
from jax.experimental import pallas as pl
from jax.experimental.pallas import tpu as pltpu
from jax.sharding import PartitionSpec as P

EPSILON = 1e-06
MESH = pl.DeviceIdType.MESH
SLICES = 4
SEGMENTS = 8
STEPS = (1, 2, 3, 4, -1, -2, -3)
GATHER_FROM = (
    {-3: -2, -2: "x", -1: "x", 0: "x", 1: "x", 2: 1, 3: "x", 4: "x"},
    {-3: -2, -2: "x", -1: -2, 0: "x", 1: "x", 2: 1, 3: "x", 4: "x"},
    {-3: -2, -2: "x", -1: "x", 0: "x", 1: 0, 2: "x", 3: "x", 4: 3},
    {-3: -2, -2: "x", -1: 0, 0: "x", 1: "x", 2: "x", 3: 1, 4: 3},
)
SCATTER_TO = (
    {-3: -2, -2: -1, -1: "x", 0: "x", 1: "x", 2: 1, 3: "x", 4: 3},
    {-3: "x", -2: -1, -1: "x", 0: "x", 1: 0, 2: "x", 3: "x", 4: "x"},
    {-3: -2, -2: "x", -1: "x", 0: "x", 1: "x", 2: "x", 3: "x", 4: 3},
    {-3: -2, -2: -1, -1: "x", 0: "x", 1: 0, 2: "x", 3: "x", 4: "x"},
)
GATHER_OWN = (
    {1: 0, 2: 1, 3: 1, 4: 3, -1: 0, -2: -1, -3: -2},
    {1: 0, 2: 1, 3: 1, 4: 3, -1: 0, -2: 0, -3: -2},
    {1: 0, 2: 1, 3: 2, 4: 3, -1: 0, -2: 0, -3: -2},
    {1: 0, 2: 1, 3: 2, 4: 3, -1: 0, -2: 0, -3: -2},
)
SCATTER_OWN = (
    {1: 0, 2: 1, 3: 1, 4: 3, -1: 0, -2: -1, -3: -2},
    {1: 0, 2: 0, 3: 2, 4: 3, -1: 0, -2: -1, -3: -2},
    {1: 0, 2: 0, 3: 2, 4: 3, -1: 0, -2: 0, -3: -2},
    {1: 0, 2: 0, 3: 2, 4: 3, -1: 0, -2: -1, -3: -2},
)
GATHER_ORDER = (
    (0, "o", 1), (0, "o", -1), (3, "o", 1), (1, "t", 0), (2, "o", 1), (1, "o", 1), (3, "o", -2), (3, "t", 0),
    (1, "o", -2), (0, "t", 0), (2, "o", -2), (2, "t", 0), (0, "t", -1), (3, "o", 2), (0, "o", -2),
    (3, "t", 1), (2, "o", 2), (1, "t", 1), (0, "t", 1), (1, "o", 3), (0, "o", 3), (3, "t", -2), (0, "o", 2),
    (2, "o", -1), (1, "t", -2), (1, "o", 2), (3, "t", -1), (3, "t", 3), (2, "o", 3), (3, "o", 3),
    (0, "t", -2), (3, "o", -3), (1, "o", 4), (0, "t", 3), (3, "o", -1), (0, "o", 4), (2, "t", -2),
    (3, "t", -3), (2, "t", 2), (1, "t", -3), (2, "t", 3), (3, "t", 4), (1, "o", -1), (3, "o", 4),
    (1, "t", 2), (1, "t", -1), (3, "t", 2), (1, "t", 3), (1, "o", -3), (0, "o", -3), (0, "t", -3),
    (1, "t", 4), (2, "o", 4), (2, "o", -3), (0, "t", 4), (0, "t", 2), (2, "t", -1), (2, "t", -3),
    (2, "t", 1), (2, "t", 4), (3, "P", 0), (1, "P", 0), (0, "P", 0), (2, "P", 0),
)
SCATTER_ORDER = (
    (2, "M", 0), (2, "t", -1), (2, "o", 4), (2, "t", 4), (2, "t", -3), (1, "M", 0), (1, "t", 4), (3, "M", 0),
    (3, "o", 1), (3, "t", 4), (2, "o", -3), (2, "t", 2), (3, "t", -3), (0, "M", 0), (1, "t", -3),
    (1, "t", -2), (0, "t", -3), (1, "t", 3), (3, "t", 3), (0, "t", 4), (0, "o", -3), (2, "o", -1),
    (3, "o", -3), (3, "t", -2), (1, "o", 4), (2, "t", 3), (3, "o", 4), (0, "o", 4), (0, "t", 3),
    (0, "t", -2), (0, "t", 2), (3, "t", 2), (3, "t", 1), (0, "o", -2), (1, "t", 2), (1, "o", -3),
    (3, "o", -2), (1, "o", 3), (0, "o", 2), (2, "t", 1), (3, "o", 3), (3, "t", -1), (1, "t", 1),
    (1, "t", -1), (2, "o", 3), (1, "o", 1), (2, "t", -2), (0, "t", 1), (1, "o", -2), (0, "o", 3),
    (0, "t", -1), (1, "o", 2), (3, "o", 2), (2, "o", 2), (3, "t", 0), (1, "t", 0), (3, "o", -1), (2, "t", 0),
    (0, "t", 0), (2, "o", 1), (2, "o", -2), (1, "o", -1), (0, "o", 1), (0, "o", -1), (1, "F", 0),
    (3, "F", 0), (2, "F", 0), (0, "F", 0),
)
SLOT = {("o", p): i for i, p in enumerate(STEPS)} | {("t", p): 7 + i for i, p in enumerate((0,) + STEPS)}
SLOTS = 15


def kernel(
    sizes,
    tokens_hbm, gain_hbm, win_hbm, taps_hbm, res_hbm, rate_hbm, skip_hbm, wout_hbm,
    out,
    tok, gain, win, taps, res, rate, skip, wout,
    xg, proj, sig, gate, dec, res3, far, step3, ends, message, messages, rows32, before, heads, decays, inc,
    gated32, gated, part, land,
    load_sem, ag_send, ag_recv, rs_send, rs_recv, st_send, st_recv,
):
    ring, n_ctx, rows, width = sizes
    block_rows = 2 * ring * rows
    cols = width // SLICES
    seg = block_rows // SEGMENTS
    channels = rate.shape[1]

    dp, ctx, tensor = lax.axis_index("dp"), lax.axis_index("ctx"), lax.axis_index("tensor")
    plane, z = tensor // ring, tensor % ring

    def at(ctx_now, plane_now, z_now):
        return (dp, ctx_now, plane_now * ring + z_now)

    partner = at(ctx, 1 - plane, z)

    loads = [
        pltpu.make_async_copy(source, target, load_sem.at[i])
        for i, (source, target) in enumerate(
            (
                (tokens_hbm, tok), (gain_hbm, gain), (rate_hbm, rate), (res_hbm, res),
                (taps_hbm, taps), (skip_hbm, skip), (win_hbm, win), (wout_hbm, wout),
            )
        )
    ]
    for load in loads:
        load.start()

    messages[...] = jnp.zeros(messages.shape, messages.dtype)
    barrier = pltpu.get_barrier_semaphore()
    peers = [partner] + [at(ctx, plane, (z + steps) % ring) for steps in (1, 2, ring - 2, ring - 1)]
    peers += [at((ctx + o) % n_ctx, plane, z) for o in range(1, n_ctx)]
    for peer in peers:
        pl.semaphore_signal(barrier, inc=1, device_id=peer, device_id_type=MESH)

    def ring_at(k, steps):
        return (z + (1 - 2 * (k % 2)) * steps + 2 * ring) % ring

    def where(kind, k, position):
        return (plane if kind == "o" else 1 - plane), ring_at(k, -position)

    def block(plane_now, z_now):
        return pl.ds(pl.multiple_of((plane_now * ring + z_now) * rows, rows), rows)

    def gather_copy(k, kind, position, source_kind, source, target):
        mine = xg.at[k, block(*where(source_kind, k, source)), :]
        slot = SLOT[kind, position]
        return pltpu.make_async_remote_copy(
            src_ref=mine, dst_ref=mine, send_sem=ag_send.at[k, slot], recv_sem=ag_recv.at[k, slot],
            device_id=target, device_id_type=MESH,
        )

    def scatter_copy(k, kind, position, target):
        slot = SLOT[kind, position]
        return pltpu.make_async_remote_copy(
            src_ref=part.at[k, block(*where(kind, k, position)), :], dst_ref=land.at[k, slot],
            send_sem=rs_send.at[k, slot], recv_sem=rs_recv.at[k, slot],
            device_id=target, device_id_type=MESH,
        )

    loads[0].wait()
    loads[1].wait()
    values = tok[...].astype(jnp.float32)
    spread = jnp.mean(values * values, axis=-1, keepdims=True)
    normed = (values * lax.rsqrt(spread + EPSILON) * gain[...]).astype(jnp.bfloat16)
    for k in range(SLICES):
        xg[k, block(plane, z), :] = normed[:, k * cols : (k + 1) * cols]
    pl.semaphore_wait(barrier, len(peers))

    got = set()

    def need(k, kind, position):
        if (k, kind, position) not in got:
            got.add((k, kind, position))
            gather_copy(k, kind, position, kind, position, partner).wait_recv()

    def send_gather(k, kind, position):
        if kind == "o":
            source = GATHER_OWN[k][position]
            if source:
                need(k, "o", source)
            gather_copy(k, "o", position, "o", source, at(ctx, plane, ring_at(k, position - source))).start()
        elif GATHER_FROM[k][position] == "x":
            if position:
                need(k, "o", position)
            gather_copy(k, "t", position, "o", position, partner).start()
        else:
            source = GATHER_FROM[k][position]
            need(k, "t", source)
            gather_copy(k, "t", position, "t", source, at(ctx, plane, ring_at(k, position - source))).start()

    first_wait = next(i for i, (k, kind, p) in enumerate(GATHER_ORDER) if (kind, p) != ("t", 0) and (kind != "o" or GATHER_OWN[k][p]))
    for step in GATHER_ORDER[:first_wait]:
        send_gather(*step)

    loads[2].wait()
    loads[3].wait()
    loads[4].wait()
    loads[5].wait()
    modes = rate.shape[0]
    for m in range(modes):
        step3[m] = jnp.broadcast_to(rate[m : m + 1, :], (SEGMENTS, channels))
        res3[m] = jnp.broadcast_to(res[m : m + 1, :], (SEGMENTS, channels))
    dec[...] = jnp.exp(-step3[...])
    far[...] = jnp.exp(step3[...] * (-float(seg)))
    segment = lax.broadcasted_iota(jnp.int32, (modes, SEGMENTS, channels), 1)
    step3[...] = jnp.exp(step3[...] * (segment.astype(jnp.float32) * (-float(seg))))
    decays[0] = jnp.exp(-rate[...])
    decays[1] = jnp.exp(rate[...] * (-float(block_rows)))
    decays[2] = jnp.exp(rate[...] * (-float(block_rows - 2)))
    decays[3] = jnp.exp(rate[...])

    def project(k):
        for p in STEPS:
            need(k, "o", p)
        for p in (0,) + STEPS:
            need(k, "t", p)
        for g in range(3):
            group = pl.ds(g * channels, channels)
            product = jnp.dot(xg[k], win[g, k * cols : (k + 1) * cols, :], preferred_element_type=jnp.float32)
            product = product.reshape(SEGMENTS, seg, channels)
            if len(projected) == 0:
                proj[:, :, group] = product
            else:
                proj[:, :, group] += product
        projected.append(k)

    projected = []
    for k, kind, position in GATHER_ORDER[first_wait:]:
        if kind == "P":
            if not projected:
                loads[6].wait()
            project(k)
        else:
            send_gather(k, kind, position)

    taps32 = taps[...].astype(jnp.float32)

    def tap(j, g):
        return taps32[j, g : g + 1, :]

    def short_mix(i, now, one, two):
        featured = []
        for g in range(3):
            group = slice(g * channels, (g + 1) * channels)
            featured.append(tap(0, g) * now[:, group] + tap(1, g) * one[:, group] + tap(2, g) * two[:, group])
        sig[i] = featured[0] * featured[2]
        gate[i] = featured[1]

    def short_step(i, carry):
        short_mix(i, proj[:, i, :], proj[:, i - 1, :], proj[:, i - 2, :])
        return carry

    lax.fori_loop(2, seg, short_step, 0, unroll=True)

    first_row = lax.broadcasted_iota(jnp.int32, (SEGMENTS, 3 * channels), 0) == 0
    first_sig = lax.broadcasted_iota(jnp.int32, (SEGMENTS, channels), 0) == 0
    row_zero, row_next = proj[:, 0, :], proj[:, 1, :]
    row_one = pltpu.roll(proj[:, seg - 1, :], 1, 0)
    row_two = pltpu.roll(proj[:, seg - 2, :], 1, 0)
    short_mix(0, row_zero, row_one, row_two)
    short_mix(1, row_next, row_zero, row_one)
    sig[0] = jnp.where(first_sig, 0.0, sig[0])
    sig[1] = jnp.where(first_sig, 0.0, sig[1])

    halves = [pl.ds(first, 128) for first in range(0, channels, 128)]
    lane = lax.broadcasted_iota(jnp.int32, (modes, SEGMENTS, 128), 1)
    for half in halves:

        def end_step(i, carry, half=half):
            return dec[:, :, half] * carry + sig[i, :, half][None]

        total = lax.fori_loop(0, seg, end_step, jnp.zeros((modes, SEGMENTS, 128), jnp.float32), unroll=True)
        leap = far[:, :, half]
        for hop in (1, 2, 4):
            total = total + jnp.where(lane >= hop, leap * pltpu.roll(total, hop, 1), 0.0)
            leap = leap * leap
        ends[:, :, half] = total

    message[0:modes, :] = ends[:, SEGMENTS - 1, :].astype(jnp.bfloat16)
    last = [proj[SEGMENTS - 1, seg - 2 : seg - 1, :], proj[SEGMENTS - 1, seg - 1 : seg, :]]
    outer = [row_zero[0:1, :], row_next[0:1, :]] + last
    rows32[...] = jnp.zeros(rows32.shape, jnp.float32)
    for r, row in enumerate(outer):
        rows32[r : r + 1, :] = row[:, 0:channels]
        rows32[4 + r : 5 + r, :] = row[:, 2 * channels :]
    for r, row in enumerate(last):
        rows32[8 + r : 9 + r, :] = row[:, channels : 2 * channels]
    message[modes:, :] = rows32[...].astype(jnp.bfloat16)
    copies = [
        pltpu.make_async_remote_copy(
            src_ref=message, dst_ref=messages.at[o - 1], send_sem=st_send.at[o - 1], recv_sem=st_recv.at[o - 1],
            device_id=at((ctx + o) % n_ctx, plane, z), device_id_type=MESH,
        )
        for o in range(1, n_ctx)
    ]
    for o, copy in enumerate(copies, 1):

        @pl.when(ctx + o < n_ctx)
        def _(copy=copy):
            copy.start()


    for half in halves:
        ends[:, :, half] = jnp.where(lane >= 1, pltpu.roll(ends[:, :, half], 1, 1), 0.0)

    for k in range(SLICES):
        for kind, position in SLOT:
            gather_copy(k, kind, position, kind, position, partner).wait_send()

    for o in range(1, n_ctx):

        @pl.when(o <= ctx)
        def _(o=o):
            copies[o - 1].wait_recv()

        before[o - 1] = messages[o - 1, modes:, :].astype(jnp.float32)
    before[n_ctx - 1] = jnp.zeros(before.shape[1:], jnp.float32)
    before[n_ctx] = jnp.zeros(before.shape[1:], jnp.float32)

    def first_two(r, g):
        start, then = before[0:n_ctx, r, :], before[0:n_ctx, r + 1, :]
        two, one = before[1 : n_ctx + 1, r + 2, :], before[1 : n_ctx + 1, r + 3, :]
        return (
            tap(0, g) * start + tap(1, g) * one + tap(2, g) * two,
            tap(0, g) * then + tap(1, g) * start + tap(2, g) * one,
        )

    left, right = first_two(0, 0), first_two(4, 2)
    heads[0] = left[0] * right[0]
    heads[1] = left[1] * right[1]
    decay = decays[0]
    incoming = jnp.zeros(rate.shape, jnp.float32)
    for o in range(n_ctx - 1, 0, -1):
        ended = messages[o - 1, 0:modes, :].astype(jnp.float32)
        head = decay * heads[0, o - 1 : o, :] + heads[1, o - 1 : o, :]
        incoming = decays[1] * incoming + (ended + decays[2] * head)

    def halo(r):
        row = jnp.concatenate([before[0, r : r + 1, :], before[0, 8 + r - 2 : 9 + r - 2, :], before[0, 4 + r : 5 + r, :]], axis=1)
        return jnp.broadcast_to(row, (SEGMENTS, 3 * channels))

    row_one = jnp.where(first_row, halo(3), pltpu.roll(proj[:, seg - 1, :], 1, 0))
    row_two = jnp.where(first_row, halo(2), pltpu.roll(proj[:, seg - 2, :], 1, 0))
    row_zero = proj[:, 0, :]
    short_mix(0, row_zero, row_one, row_two)
    short_mix(1, proj[:, 1, :], row_zero, row_one)
    inc[0] = incoming
    inc[1] = incoming + decays[3] * (sig[0, 0:1, :] + decays[3] * sig[1, 0:1, :])
    first_sig = lax.broadcasted_iota(jnp.int32, (SEGMENTS, channels), 0) == 0
    for m in range(modes):
        ends[m] = ends[m] + step3[m] * jnp.where(first_sig, inc[0, m : m + 1, :], inc[1, m : m + 1, :])

    for half in halves:

        def long_step(i, carry, half=half):
            now = sig[i, :, half]
            carry = dec[:, :, half] * carry + now[None]
            mixed = jnp.sum(res3[:, :, half] * carry, axis=0)
            gated32[i, :, half] = gate[i, :, half] * (mixed + skip[:, half] * now)
            return carry

        lax.fori_loop(0, seg, long_step, ends[:, :, half], unroll=True)
    for s in range(SEGMENTS):
        gated[s * seg : (s + 1) * seg, :] = gated32[:, s, :].astype(jnp.bfloat16)

    loads[7].wait()

    def add(k, kind, position, terms):
        for term in terms:
            scatter_copy(k, *term, partner).wait_recv()
        mine = block(*where(kind, k, position))
        total = part[k, mine, :].astype(jnp.float32)
        for term in terms:
            total = total + land[k, SLOT[term]].astype(jnp.float32)
        return mine, total

    def terms_of(k, kind, position):
        terms = [("t", p) for p in STEPS if kind == "t" and SCATTER_TO[k][p] == position]
        if kind == "o":
            terms += [("o", p) for p in STEPS if SCATTER_OWN[k][p] == position]
            terms += [("t", position)] if SCATTER_TO[k][position] == "x" else []
        return terms

    def send_scatter(k, kind, position):
        terms = terms_of(k, kind, position)
        if terms:
            mine, total = add(k, kind, position, terms)
            part[k, mine, :] = total.astype(jnp.bfloat16)
        target = (SCATTER_OWN if kind == "o" else SCATTER_TO)[k][position]
        device = partner if target == "x" else at(ctx, plane, ring_at(k, target - position))
        scatter_copy(k, kind, position, device).start()

    def drain(k, kinds):
        for kind, position in kinds:
            scatter_copy(k, kind, position, partner).wait_send()

    finished = []
    for k, kind, position in SCATTER_ORDER:
        columns = slice(k * cols, (k + 1) * cols)
        if kind == "M":
            product = jnp.dot(gated[...], wout[:, columns], preferred_element_type=jnp.float32)
            part[k] = product.astype(jnp.bfloat16)
        elif kind == "F":
            drain(k, [other for other in SLOT if other not in terms_of(k, "o", 0)])
            _, total = add(k, "o", 0, terms_of(k, "o", 0))
            out[:, columns] = (total + tok[:, columns].astype(jnp.float32)).astype(jnp.bfloat16)
        else:
            send_scatter(k, kind, position)
    for k in range(SLICES):
        drain(k, terms_of(k, "o", 0))
    for o, copy in enumerate(copies, 1):

        @pl.when(ctx + o < n_ctx)
        def _(copy=copy):
            copy.wait_send()


def on_device(ring, n_ctx, tokens, norm_gain, in_weight, short_filter, residues, decay_rate, skip_gain, out_weight):
    rows, width = tokens.shape
    modes, channels = decay_rate.shape
    block_rows = 2 * ring * rows
    seg = block_rows // SEGMENTS
    cols = width // SLICES
    f32, bf16 = jnp.float32, jnp.bfloat16
    any_spec = pl.BlockSpec(memory_space=pl.ANY)
    table = pltpu.VMEM((modes, SEGMENTS, channels), f32)
    dma = pltpu.SemaphoreType.DMA
    return pl.pallas_call(
        functools.partial(kernel, (ring, n_ctx, rows, width)),
        out_shape=pltpu.VMEM((rows, width), bf16),
        in_specs=[any_spec] * 8,
        out_specs=pl.BlockSpec(memory_space=pltpu.VMEM),
        scratch_shapes=[
            pltpu.VMEM((rows, width), bf16),
            pltpu.VMEM((1, width), f32),
            pltpu.VMEM((3, width, channels), bf16),
            pltpu.VMEM(short_filter.shape, bf16),
            pltpu.VMEM((modes, channels), f32),
            pltpu.VMEM((modes, channels), f32),
            pltpu.VMEM((1, channels), f32),
            pltpu.VMEM((channels, width), bf16),
            pltpu.VMEM((SLICES, block_rows, cols), bf16),
            pltpu.VMEM((SEGMENTS, seg, 3 * channels), f32),
            pltpu.VMEM((seg, SEGMENTS, channels), f32),
            pltpu.VMEM((seg, SEGMENTS, channels), f32),
            table, table, table, table, table,
            pltpu.VMEM((modes + 16, channels), bf16),
            pltpu.VMEM((n_ctx - 1, modes + 16, channels), bf16),
            pltpu.VMEM((16, channels), f32),
            pltpu.VMEM((n_ctx + 1, 16, channels), f32),
            pltpu.VMEM((2, n_ctx, channels), f32),
            pltpu.VMEM((4, modes, channels), f32),
            pltpu.VMEM((2, modes, channels), f32),
            pltpu.VMEM((seg, SEGMENTS, channels), f32),
            pltpu.VMEM((block_rows, channels), bf16),
            pltpu.VMEM((SLICES, block_rows, cols), bf16),
            pltpu.VMEM((SLICES, SLOTS, rows, cols), bf16),
            dma((8,)),
            dma((SLICES, SLOTS)), dma((SLICES, SLOTS)),
            dma((SLICES, SLOTS)), dma((SLICES, SLOTS)),
            dma((n_ctx - 1,)), dma((n_ctx - 1,)),
        ],
        name="hyena_layer",
        cost_estimate=pl.CostEstimate(
            flops=2 * block_rows * width * channels * 4, bytes_accessed=8 * width * channels, transcendentals=0
        ),
        compiler_params=pltpu.CompilerParams(
            collective_id=0, has_side_effects=True, vmem_limit_bytes=60 * 2**20
        ),
    )(
        tokens, norm_gain.reshape(1, width), in_weight.transpose(1, 0, 2), short_filter,
        residues, decay_rate, skip_gain.reshape(1, channels), out_weight,
    )


def solution(mesh):
    ring, n_ctx = mesh.shape["tensor"] // 2, mesh.shape["ctx"]
    in_specs = (
        P(("dp", "ctx", "tensor"), None),
        P(),
        P(None, None, "tensor"),
        P(None, None, "tensor"),
        P(None, "tensor"),
        P(None, "tensor"),
        P("tensor"),
        P("tensor", None),
    )
    out_specs = P(("dp", "ctx", "tensor"), None)
    return jax.shard_map(
        functools.partial(on_device, ring, n_ctx),
        mesh=mesh, in_specs=in_specs, out_specs=out_specs, check_vma=False,
    )
```
